256 devices in a mesh: gx: 8 (over z), gy: 32 (over x, y, core).
Axes of the slice: x: 4, y: 4, z: 8, core: 2. Of those that a mesh axis runs over, the one named last changes fastest.
Arguments:
- archive: bfloat16 [1048576, 1024], P(('gx', 'gy')), may hold values from -100 to 100
- sketch: bfloat16 [1024, 256], replicated, may hold values from -0.1875 to 0.1875
Outputs:
- q_rows: bfloat16 [1048576, 256], P(('gx', 'gy'))
- r_factor: float32 [256, 256], replicated
- projection: float32 [1024, 256], P(('gx', 'gy'))
The draws below stay inside these ranges and needn't reach their ends.
All inputs are finite; a program needn't handle non-finite values.
Results may differ from the reference program's by a relative error of at most 0.0012.
Values sent between devices are 32-bit elements; how exact they have to be, the bound alone decides.
A program may use at most 64 MiB of HBM per device.

```python
import jax
import jax.numpy as jnp
from jax import lax

DEKADS = 1024
RANK = 256
PIXELS = 1048576


def draw_archive(key, part):
    key = jax.random.fold_in(key, 1)
    first, second, third = jax.random.split(key, 3)
    trend = jnp.exp(jnp.log(3.0) * jnp.arange(PIXELS, dtype=jnp.float32) / PIXELS)[:, None]
    row_scale = jnp.exp(jnp.log(10.0) * jax.random.uniform(first, (PIXELS, 1), jnp.float32)) * trend
    col_scale = jnp.exp(jnp.log(10.0) * jax.random.uniform(second, (1, DEKADS), jnp.float32))
    base = jnp.clip(jax.random.normal(third, (PIXELS, DEKADS), jnp.float32), -6.0, 6.0)
    return (base * row_scale * col_scale / 20.0).astype(jnp.bfloat16)


def noise(stream_key, shape, width, limit, held_as=jnp.bfloat16):
    return jnp.clip(width * jax.random.normal(stream_key, shape, jnp.float32), -limit, limit).astype(held_as)


def setup_inputs(seed: int = 0) -> dict:
    arg_keys = jax.random.split(jax.random.key(seed), 3)
    archive = draw_archive(jax.random.fold_in(arg_keys[2], 71), 0)
    sketch = noise(arg_keys[1], (DEKADS, RANK), DEKADS ** -0.5, 0.1875)
    return dict(archive=archive, sketch=sketch)


def reference(archive, sketch):
    sketched = jnp.dot(archive.astype(jnp.float32), sketch.astype(jnp.float32), preferred_element_type=jnp.float32)
    gram = jnp.dot(sketched.T, sketched, precision=lax.Precision.HIGHEST)
    lower = jnp.linalg.cholesky(gram) / jnp.sqrt(jnp.float32(PIXELS))
    r_factor = lower.T
    q_rows = jax.scipy.linalg.solve_triangular(lower, sketched.T, lower=True).T.astype(jnp.bfloat16)
    projection = jnp.einsum('pd,pk->dk', archive.astype(jnp.float32), q_rows.astype(jnp.float32), preferred_element_type=jnp.float32) / jnp.sqrt(jnp.float32(PIXELS))
    return (q_rows, r_factor, projection)
```

```python
import functools

import jax
import jax.numpy as jnp
from jax import lax
from jax.experimental import pallas as pl
from jax.experimental.pallas import tpu as pltpu
from jax.sharding import PartitionSpec as P

F32, BF16 = jnp.float32, jnp.bfloat16
PARTS = 8
MESH = pl.DeviceIdType.MESH
NT = (((1,), (1,)), ((), ()))


def dot(a, b):
    return jnp.dot(a, b, preferred_element_type=F32)


def dot_nt(a, b):
    return lax.dot_general(a, b, NT, preferred_element_type=F32)


def pieces(value):
    high = value.astype(BF16)
    rest = value - high.astype(F32)
    middle = rest.astype(BF16)
    return high, middle, (rest - middle.astype(F32)).astype(BF16)


def exchange(
    archive_hbm, sketch_hbm, gram_ref, s_hbm, w_ref,
    a, sk, s, hm, acc, wt, g, gcore, gxy, gz, gsum, w, wcore, wxy, wz, wtile,
    a_sem, s_sem, sk_sem, send1, recv1, send2, recv2, send3, recv3, send4, recv4,
    send5, recv5, wsend1, wrecv1, wsend2, wrecv2, wsend3, wrecv3,
):
    z, gy = lax.axis_index("gx"), lax.axis_index("gy")
    core, xy = gy % 2, gy // 2
    rows = a.shape[1]

    def device(zz, xx, cc):
        return (zz, xx * 2 + cc)

    def load(i):
        return pltpu.make_async_copy(
            archive_hbm.at[pl.ds(pl.multiple_of(i * rows, rows), rows), :], a.at[i], a_sem.at[i]
        )

    def save(i):
        return pltpu.make_async_copy(
            s.at[i], s_hbm.at[pl.ds(pl.multiple_of(i * rows, rows), rows), :], s_sem.at[i]
        )

    load_sketch = pltpu.make_async_copy(sketch_hbm, sk, sk_sem)
    load_sketch.start()
    for i in range(PARTS):
        load(i).start()

    barrier = pltpu.get_barrier_semaphore()
    for o in range(1, 16):
        pl.semaphore_signal(barrier, inc=1, device_id=device(z, (xy + o) % 16, core), device_id_type=MESH)
    for o in range(1, 16):
        line = (z * 2 + core + o) % 16
        pl.semaphore_signal(barrier, inc=1, device_id=device(line // 2, xy, line % 2), device_id_type=MESH)

    acc[...] = jnp.zeros_like(acc)
    load_sketch.wait()

    def part(i, carry):
        load(i).wait()
        block = dot(a[i], sk[...])
        s[i] = block
        save(i).start()
        high, middle, low = pieces(block.T)
        hm[i, :256] = high
        hm[i, 256:] = middle
        acc[:768] += dot_nt(jnp.concatenate([high, middle, low], axis=0), high)
        acc[768:] += dot_nt(middle, middle)
        return carry

    lax.fori_loop(0, PARTS, part, 0)
    mixed = acc[256:512] + acc[512:768]
    g[...] = ((acc[:256] + acc[768:]) + (mixed + mixed.T)).reshape(32, 8, 256)

    def remote(src, dst, send, recv, to):
        return pltpu.make_async_remote_copy(
            src_ref=src, dst_ref=dst, send_sem=send, recv_sem=recv, device_id=to, device_id_type=MESH
        )

    other = 1 - core
    sibling = device(z, xy, other)

    def half(ref, which, size):
        return ref.at[pl.ds(pl.multiple_of(which * size, size), size)]

    def cross(b):
        wt[...] = jnp.zeros_like(wt)
        columns = pl.ds(pl.multiple_of(b * 256, 256), 256)

        def step(i, carry):
            both = dot(hm[i], a[i, :, columns])
            wt[...] += both[:256] + both[256:]
            return carry

        lax.fori_loop(0, PARTS, step, 0)
        w[pl.ds(pl.multiple_of(b * 32, 32), 32)] = wt[...].T.reshape(32, 8, 256)

    pl.semaphore_wait(barrier, 30)
    one = remote(half(g, other, 16), gcore, send1, recv1, sibling)
    one.start()
    cross(other * 2)
    one.wait()
    gcore[...] += half(g, core, 16)[...]

    def two(o):
        to = (xy + o) % 16
        return remote(gcore.at[to], gxy.at[o], send2.at[o], recv2.at[o], device(z, to, core))

    for o in range(1, 16):
        two(o).start()
    cross(other * 2 + 1)
    wone = remote(half(w, other, 64), wcore, wsend1, wrecv1, sibling)
    total = gcore[xy]
    for o in range(1, 16):
        two(o).wait_recv()
        total += gxy[o]
    gz[z] = total

    def three(o):
        return remote(gz.at[z], gz.at[z], send3.at[o], recv3.at[z], device((z + o) % 8, xy, core))

    def three_in(o):
        slot = (z + o) % 8
        return remote(gz.at[slot], gz.at[slot], send3.at[o], recv3.at[slot], device(slot, xy, core))

    for o in range(1, 8):
        three(o).start()
    wone.start()
    cross(core * 2)
    for o in range(1, 8):
        three_in(o).wait_recv()
    total = gz[0]
    for o in range(1, 8):
        total += gz[o]
    mine = core * 16 + xy
    gsum[mine] = total

    def four(o):
        return remote(
            gsum.at[mine], gsum.at[mine], send4.at[o], recv4.at[xy], device(z, (xy + o) % 16, core)
        )

    def four_in(o):
        slot = (xy + o) % 16
        there = gsum.at[core * 16 + slot]
        return remote(there, there, send4.at[o], recv4.at[slot], device(z, slot, core))

    for o in range(1, 16):
        four(o).start()
    cross(core * 2 + 1)
    for o in range(1, 16):
        four_in(o).wait_recv()

    five = remote(half(gsum, core, 16), half(gsum, core, 16), send5, recv5, sibling)
    five_in = remote(half(gsum, other, 16), half(gsum, other, 16), send5, recv5, sibling)
    five.start()

    wone.wait()
    wcore[...] += half(w, core, 64)[...]
    for t in range(4):
        for i in range(16):
            wtile[i, t] = wcore[t * 16 + i]

    def wtwo(o):
        to = (xy + o) % 16
        return remote(wtile.at[to], wxy.at[o], wsend2.at[o], wrecv2.at[o], device(z, to, core))

    for o in range(1, 16):
        wtwo(o).start()
    five_in.wait_recv()
    wsum = wtile[xy]
    for o in range(1, 16):
        wtwo(o).wait_recv()
        wsum += wxy[o]
    wcore[:4] = wsum

    def wthree(t, cc):
        to = core * 4 + t
        return remote(
            wcore.at[t], wz.at[z], wsend3.at[t * 2 + cc], wrecv3.at[z], device(to, xy, cc)
        )

    owner = z // 4
    for t in range(4):
        for cc in range(2):
            here = jnp.logical_and(z == core * 4 + t, core == cc)

            @pl.when(jnp.logical_not(here))
            def _():
                wthree(t, cc).start()

            @pl.when(here)
            def _():
                wz[z] = wcore[t]

    for zz in range(8):
        own = jnp.logical_and(z == zz, core == owner)

        @pl.when(jnp.logical_not(own))
        def _():
            remote(
                wcore.at[0], wz.at[zz], wsend3.at[0], wrecv3.at[zz], device(zz, xy, owner)
            ).wait_recv()

    total = wz[0]
    for zz in range(1, 8):
        total += wz[zz]
    w_ref[...] = total
    gram_ref[...] = gsum[...].reshape(256, 256)

    for o in range(1, 16):
        two(o).wait_send()
        four(o).wait_send()
        wtwo(o).wait_send()
    for o in range(1, 8):
        three(o).wait_send()
    five.wait_send()
    for t in range(4):
        for cc in range(2):

            @pl.when(jnp.logical_not(jnp.logical_and(z == core * 4 + t, core == cc)))
            def _():
                wthree(t, cc).wait_send()

    for i in range(PARTS):
        save(i).wait()


def local(archive, sketch):
    pixels, depth = archive.shape
    rank = sketch.shape[1]
    rows = pixels // PARTS
    any_spec = pl.BlockSpec(memory_space=pl.ANY)
    vmem = pl.BlockSpec(memory_space=pltpu.VMEM)
    dma = pltpu.SemaphoreType.DMA
    gram, s, w8 = pl.pallas_call(
        exchange,
        out_shape=(
            jax.ShapeDtypeStruct((rank, rank), F32),
            jax.ShapeDtypeStruct((pixels, rank), F32),
            jax.ShapeDtypeStruct((8, rank), F32),
        ),
        in_specs=[any_spec, any_spec],
        out_specs=(vmem, any_spec, vmem),
        scratch_shapes=[
            pltpu.VMEM((PARTS, rows, depth), BF16),
            pltpu.VMEM((depth, rank), BF16),
            pltpu.VMEM((PARTS, rows, rank), F32),
            pltpu.VMEM((PARTS, 512, rows), BF16),
            pltpu.VMEM((1024, 256), F32),
            pltpu.VMEM((256, 256), F32),
            pltpu.VMEM((32, 8, 256), F32),
            pltpu.VMEM((16, 8, 256), F32),
            pltpu.VMEM((16, 8, 256), F32),
            pltpu.VMEM((8, 8, 256), F32),
            pltpu.VMEM((32, 8, 256), F32),
            pltpu.VMEM((128, 8, 256), F32),
            pltpu.VMEM((64, 8, 256), F32),
            pltpu.VMEM((16, 4, 8, 256), F32),
            pltpu.VMEM((8, 8, 256), F32),
            pltpu.VMEM((16, 4, 8, 256), F32),
            dma((PARTS,)), dma((PARTS,)), dma, dma, dma, dma((16,)), dma((16,)),
            dma((8,)), dma((8,)), dma((16,)), dma((16,)), dma, dma,
            dma, dma, dma((16,)), dma((16,)), dma((8,)), dma((8,)),
        ],
        compiler_params=pltpu.CompilerParams(
            collective_id=0, has_side_effects=True, vmem_limit_bytes=48 * 2**20
        ),
    )(archive, sketch)
    root = jnp.sqrt(F32(pixels * lax.axis_size("gx") * lax.axis_size("gy")))
    lower = jnp.linalg.cholesky(gram) / root
    q_rows = jax.scipy.linalg.solve_triangular(lower, s.T, lower=True).T.astype(BF16)
    both = jax.scipy.linalg.solve_triangular(lower, w8.T, lower=True).T / root
    projection = lax.dynamic_slice_in_dim(both, (lax.axis_index("gy") % 2) * 4, 4, 0)
    return q_rows, lower.T, projection


def solution(mesh):
    return jax.shard_map(
        local,
        mesh=mesh,
        in_specs=(P(("gx", "gy"), None), P()),
        out_specs=(P(("gx", "gy"), None), P(), P(("gx", "gy"), None)),
        check_vma=False,
    )
```

```python
import functools

import jax
import jax.numpy as jnp
from jax import lax
from jax.experimental import pallas as pl
from jax.experimental.pallas import tpu as pltpu
from jax.sharding import PartitionSpec as P

F32, BF16 = jnp.float32, jnp.bfloat16
PARTS = 8
MESH = pl.DeviceIdType.MESH
NT = (((1,), (1,)), ((), ()))
TN = (((0,), (0,)), ((), ()))


def dot(a, b):
    return jnp.dot(a, b, preferred_element_type=F32)


def dot_nt(a, b):
    return lax.dot_general(a, b, NT, preferred_element_type=F32)


def pieces(value):
    high = value.astype(BF16)
    rest = value - high.astype(F32)
    middle = rest.astype(BF16)
    return high, middle, (rest - middle.astype(F32)).astype(BF16)


def exchange(
    archive_hbm, sketch_hbm, gram_ref, s_hbm, w_ref,
    a, sk, s, hm, acc, wt, g, gcore, gxy, gz, gsum, w, wcore, wxy, wz, wtile,
    a_sem, s_sem, sk_sem, send1, recv1, send2, recv2, send3, recv3, send4, recv4,
    send5, recv5, wsend1, wrecv1, wsend2, wrecv2, wsend3, wrecv3,
):
    z, gy = lax.axis_index("gx"), lax.axis_index("gy")
    core, xy = gy % 2, gy // 2
    rows = a.shape[1]

    def device(zz, xx, cc):
        return (zz, xx * 2 + cc)

    def load(i):
        return pltpu.make_async_copy(
            archive_hbm.at[pl.ds(pl.multiple_of(i * rows, rows), rows), :], a.at[i], a_sem.at[i]
        )

    def save(i):
        return pltpu.make_async_copy(
            s.at[i], s_hbm.at[pl.ds(pl.multiple_of(i * rows, rows), rows), :], s_sem.at[i]
        )

    load_sketch = pltpu.make_async_copy(sketch_hbm, sk, sk_sem)
    load_sketch.start()
    for i in range(PARTS):
        load(i).start()

    barrier = pltpu.get_barrier_semaphore()
    for o in range(1, 16):
        pl.semaphore_signal(barrier, inc=1, device_id=device(z, (xy + o) % 16, core), device_id_type=MESH)
    for o in range(1, 16):
        line = (z * 2 + core + o) % 16
        pl.semaphore_signal(barrier, inc=1, device_id=device(line // 2, xy, line % 2), device_id_type=MESH)

    acc[...] = jnp.zeros_like(acc)
    load_sketch.wait()

    def part(i, carry):
        load(i).wait()
        block = dot(a[i], sk[...])
        s[i] = block
        save(i).start()
        high, middle, low = pieces(block.T)
        hm[i, :256] = high
        hm[i, 256:] = middle
        acc[:768] += dot_nt(jnp.concatenate([high, middle, low], axis=0), high)
        acc[768:] += dot_nt(middle, middle)
        return carry

    lax.fori_loop(0, PARTS, part, 0)
    mixed = acc[256:512] + acc[512:768]
    g[...] = ((acc[:256] + acc[768:]) + (mixed + mixed.T)).reshape(32, 8, 256)

    def remote(src, dst, send, recv, to):
        return pltpu.make_async_remote_copy(
            src_ref=src, dst_ref=dst, send_sem=send, recv_sem=recv, device_id=to, device_id_type=MESH
        )

    other = 1 - core
    sibling = device(z, xy, other)

    def half(ref, which, size):
        return ref.at[pl.ds(pl.multiple_of(which * size, size), size)]

    def cross(b):
        wt[...] = jnp.zeros_like(wt)
        columns = pl.ds(pl.multiple_of(b * 256, 256), 256)

        def step(i, carry):
            both = dot(hm[i], a[i, :, columns])
            wt[...] += both[:256] + both[256:]
            return carry

        lax.fori_loop(0, PARTS, step, 0)
        w[pl.ds(pl.multiple_of(b * 32, 32), 32)] = wt[...].T.reshape(32, 8, 256)

    pl.semaphore_wait(barrier, 30)
    one = remote(half(g, other, 16), gcore, send1, recv1, sibling)
    one.start()
    cross(other * 2)
    one.wait()
    gcore[...] += half(g, core, 16)[...]

    def two(o):
        to = (xy + o) % 16
        return remote(gcore.at[to], gxy.at[o], send2.at[o], recv2.at[o], device(z, to, core))

    for o in range(1, 16):
        two(o).start()
    cross(other * 2 + 1)
    wone = remote(half(w, other, 64), wcore, wsend1, wrecv1, sibling)
    total = gcore[xy]
    for o in range(1, 16):
        two(o).wait_recv()
        total += gxy[o]
    gz[z] = total

    def three(o):
        return remote(gz.at[z], gz.at[z], send3.at[o], recv3.at[z], device((z + o) % 8, xy, core))

    def three_in(o):
        slot = (z + o) % 8
        return remote(gz.at[slot], gz.at[slot], send3.at[o], recv3.at[slot], device(slot, xy, core))

    for o in range(1, 8):
        three(o).start()
    wone.start()
    cross(core * 2)
    for o in range(1, 8):
        three_in(o).wait_recv()
    total = gz[0]
    for o in range(1, 8):
        total += gz[o]
    mine = core * 16 + xy
    gsum[mine] = total

    def four(o):
        return remote(
            gsum.at[mine], gsum.at[mine], send4.at[o], recv4.at[xy], device(z, (xy + o) % 16, core)
        )

    def four_in(o):
        slot = (xy + o) % 16
        there = gsum.at[core * 16 + slot]
        return remote(there, there, send4.at[o], recv4.at[slot], device(z, slot, core))

    for o in range(1, 16):
        four(o).start()
    cross(core * 2 + 1)
    for o in range(1, 16):
        four_in(o).wait_recv()

    five = remote(half(gsum, core, 16), half(gsum, core, 16), send5, recv5, sibling)
    five_in = remote(half(gsum, other, 16), half(gsum, other, 16), send5, recv5, sibling)
    five.start()

    wone.wait()
    wcore[...] += half(w, core, 64)[...]
    for t in range(4):
        for i in range(16):
            wtile[i, t] = wcore[t * 16 + i]

    def wtwo(o):
        to = (xy + o) % 16
        return remote(wtile.at[to], wxy.at[o], wsend2.at[o], wrecv2.at[o], device(z, to, core))

    for o in range(1, 16):
        wtwo(o).start()
    five_in.wait_recv()
    wsum = wtile[xy]
    for o in range(1, 16):
        wtwo(o).wait_recv()
        wsum += wxy[o]
    wcore[:4] = wsum

    def wthree(t, cc):
        to = core * 4 + t
        return remote(
            wcore.at[t], wz.at[z], wsend3.at[t * 2 + cc], wrecv3.at[z], device(to, xy, cc)
        )

    owner = z // 4
    for t in range(4):
        for cc in range(2):
            here = jnp.logical_and(z == core * 4 + t, core == cc)

            @pl.when(jnp.logical_not(here))
            def _():
                wthree(t, cc).start()

            @pl.when(here)
            def _():
                wz[z] = wcore[t]

    for zz in range(8):
        own = jnp.logical_and(z == zz, core == owner)

        @pl.when(jnp.logical_not(own))
        def _():
            remote(
                wcore.at[0], wz.at[zz], wsend3.at[0], wrecv3.at[zz], device(zz, xy, owner)
            ).wait_recv()

    total = wz[0]
    for zz in range(1, 8):
        total += wz[zz]
    w_ref[...] = jnp.where(core == 0, total[:4], total[4:])
    gram_ref[...] = gsum[...].reshape(256, 256)

    for o in range(1, 16):
        two(o).wait_send()
        four(o).wait_send()
        wtwo(o).wait_send()
    for o in range(1, 8):
        three(o).wait_send()
    five.wait_send()
    for t in range(4):
        for cc in range(2):

            @pl.when(jnp.logical_not(jnp.logical_and(z == core * 4 + t, core == cc)))
            def _():
                wthree(t, cc).wait_send()

    for i in range(PARTS):
        save(i).wait()


def row(tile, j):
    return jnp.broadcast_to(tile[j : j + 1, :], (8, 128))


def column(tile, k):
    return jnp.broadcast_to(tile[:, k : k + 1], (8, 128))


def factor(m):
    sublane = lax.broadcasted_iota(jnp.int32, (8, 128), 0)
    for top in range(0, 256, 64):
        tiles = [0, 1, 2] if top < 128 else [1, 2, 3]
        at = tiles.index(top // 128)

        def place(g, t):
            return slice(top + 8 * g, top + 8 * g + 8), slice(128 * t, 128 * t + 128)

        r = [[m[place(g, t)] for t in tiles] for g in range(8)]
        for s in range(8):
            lane = (top + 8 * s) % 128
            c = {(g, k): column(r[g][at], lane + k) for g in range(s, 8) for k in range(8)}
            scale = jnp.zeros((8, 128), F32)
            for j in range(8):
                pivot = row(c[s, j], j)
                inverse = 1.0 / pivot
                scale = jnp.where(sublane == j, lax.rsqrt(pivot), scale)
                for g in range(s, 8):
                    c[g, j] = c[g, j] * inverse
                below = jnp.where(sublane > j, c[s, j], 0.0)
                for k in range(j + 1, 8):
                    across = row(c[s, k], j)
                    for g in range(s, 8):
                        c[g, k] = c[g, k] - c[g, j] * across
                for t in range(3):
                    across = row(r[s][t], j)
                    r[s][t] = r[s][t] - below * across
                    for g in range(s + 1, 8):
                        r[g][t] = r[g][t] - c[g, j] * across
            for t in range(3):
                r[s][t] = r[s][t] * scale
        for g in range(8):
            for i, t in enumerate(tiles):
                m[place(g, t)] = r[g][i]
        low = top + 64
        if low < 256:
            width = slice(128 * tiles[0], 128 * tiles[0] + 384)
            hl, ml, ll = pieces(m[top:low, low // 128 * 128 : 256])
            hp, mp, lp = pieces(m[top:low, width])
            update = lax.dot_general(
                jnp.concatenate([hl, hl, ml, ml], axis=0),
                jnp.concatenate([hp, mp, hp, mp], axis=0),
                TN, preferred_element_type=F32,
            )
            update += lax.dot_general(
                jnp.concatenate([hl, ll], axis=0), jnp.concatenate([lp, hp], axis=0), TN, preferred_element_type=F32
            )
            m[low:, width] -= update[low % 128 :]


def finish(root, gram_ref, s_hbm, w_ref, q_hbm, r_ref, p_ref, m, s, q, s_sem, q_sem):
    rows = s.shape[1]

    def load(i):
        return pltpu.make_async_copy(s_hbm.at[pl.ds(i * rows, rows), :], s.at[i], s_sem.at[i])

    def save(i):
        return pltpu.make_async_copy(q.at[i], q_hbm.at[pl.ds(i * rows, rows), :], q_sem.at[i])

    for i in range(PARTS):
        load(i).start()
    above = lax.broadcasted_iota(jnp.int32, (256, 256), 1) - lax.broadcasted_iota(jnp.int32, (256, 256), 0)
    m[:, :256] = gram_ref[...]
    m[:, 256:] = jnp.where(above == 0, 1.0, 0.0)
    factor(m)
    inverse = jnp.where(above <= 0, m[:, 256:], 0.0)
    high, middle, _ = pieces(inverse * root)
    both = jnp.concatenate([high, middle, high], axis=1)
    for i in range(PARTS):
        load(i).wait()
        first, second, _ = pieces(s[i])
        q[i] = dot_nt(jnp.concatenate([first, first, second], axis=1), both).astype(BF16)
        save(i).start()
    r_ref[...] = jnp.where(above >= 0, m[:, :256] / root, 0.0)
    p_ref[...] = lax.dot_general(
        w_ref[...], inverse, NT, precision=lax.Precision.HIGHEST, preferred_element_type=F32
    )
    for i in range(PARTS):
        save(i).wait()


def local(archive, sketch):
    pixels, depth = archive.shape
    rank = sketch.shape[1]
    rows = pixels // PARTS
    any_spec = pl.BlockSpec(memory_space=pl.ANY)
    vmem = pl.BlockSpec(memory_space=pltpu.VMEM)
    dma = pltpu.SemaphoreType.DMA
    gram, s, w4 = pl.pallas_call(
        exchange,
        out_shape=(
            jax.ShapeDtypeStruct((rank, rank), F32),
            jax.ShapeDtypeStruct((pixels, rank), F32),
            jax.ShapeDtypeStruct((4, rank), F32),
        ),
        in_specs=[any_spec, any_spec],
        out_specs=(vmem, any_spec, vmem),
        scratch_shapes=[
            pltpu.VMEM((PARTS, rows, depth), BF16),
            pltpu.VMEM((depth, rank), BF16),
            pltpu.VMEM((PARTS, rows, rank), F32),
            pltpu.VMEM((PARTS, 512, rows), BF16),
            pltpu.VMEM((1024, 256), F32),
            pltpu.VMEM((256, 256), F32),
            pltpu.VMEM((32, 8, 256), F32),
            pltpu.VMEM((16, 8, 256), F32),
            pltpu.VMEM((16, 8, 256), F32),
            pltpu.VMEM((8, 8, 256), F32),
            pltpu.VMEM((32, 8, 256), F32),
            pltpu.VMEM((128, 8, 256), F32),
            pltpu.VMEM((64, 8, 256), F32),
            pltpu.VMEM((16, 4, 8, 256), F32),
            pltpu.VMEM((8, 8, 256), F32),
            pltpu.VMEM((16, 4, 8, 256), F32),
            dma((PARTS,)), dma((PARTS,)), dma, dma, dma, dma((16,)), dma((16,)),
            dma((8,)), dma((8,)), dma((16,)), dma((16,)), dma, dma,
            dma, dma, dma((16,)), dma((16,)), dma((8,)), dma((8,)),
        ],
        compiler_params=pltpu.CompilerParams(
            collective_id=0, has_side_effects=True, vmem_limit_bytes=48 * 2**20
        ),
    )(archive, sketch)
    root = float(pixels * lax.axis_size("gx") * lax.axis_size("gy")) ** 0.5
    return pl.pallas_call(
        functools.partial(finish, root),
        out_shape=(
            jax.ShapeDtypeStruct((pixels, rank), BF16),
            jax.ShapeDtypeStruct((rank, rank), F32),
            jax.ShapeDtypeStruct((4, rank), F32),
        ),
        in_specs=[vmem, any_spec, vmem],
        out_specs=(any_spec, vmem, vmem),
        scratch_shapes=[
            pltpu.VMEM((rank, 2 * rank), F32),
            pltpu.VMEM((PARTS, rows, rank), F32),
            pltpu.VMEM((PARTS, rows, rank), BF16),
            dma((PARTS,)), dma((PARTS,)),
        ],
        compiler_params=pltpu.CompilerParams(vmem_limit_bytes=48 * 2**20),
    )(gram, s, w4)


def solution(mesh):
    return jax.shard_map(
        local,
        mesh=mesh,
        in_specs=(P(("gx", "gy"), None), P()),
        out_specs=(P(("gx", "gy"), None), P(), P(("gx", "gy"), None)),
        check_vma=False,
    )
```

```python
import functools

import jax
import jax.numpy as jnp
from jax import lax
from jax.experimental import pallas as pl
from jax.experimental.pallas import tpu as pltpu
from jax.sharding import PartitionSpec as P

F32, BF16 = jnp.float32, jnp.bfloat16
PARTS = 2
CHUNKS = 4
MESH = pl.DeviceIdType.MESH
NT = (((1,), (1,)), ((), ()))
TN = (((0,), (0,)), ((), ()))


def dot(a, b):
    return jnp.dot(a, b, preferred_element_type=F32)


def dot_nt(a, b):
    return lax.dot_general(a, b, NT, preferred_element_type=F32)


def pieces(value):
    high = value.astype(BF16)
    rest = value - high.astype(F32)
    middle = rest.astype(BF16)
    return high, middle, (rest - middle.astype(F32)).astype(BF16)


PLANE = sorted(((i // 4, i % 4) for i in range(1, 16)), key=lambda o: -min(o[0], 4 - o[0]) - min(o[1], 4 - o[1]))
LINE = sorted(range(1, 8), key=lambda o: -min(o, 8 - o))


def exchange(
    root, archive_hbm, sketch_hbm, s_hbm, inverse_ref, r_ref, p_ref,
    a, sk, s, hm, g, gcore, gxy, gz, gsum, w, wcore, wtile, wxy, wsum, wz, m,
    a_sem, s_sem, sk_sem, send1, recv1, send2, recv2, send3, recv3, send4, recv4,
    send5, recv5, wsend1, wrecv1, wsend2, wrecv2, wsend3, wrecv3,
):
    z, gy = lax.axis_index("gx"), lax.axis_index("gy")
    core, xy = gy % 2, gy // 2
    x, y = xy // 4, xy % 4
    other = 1 - core
    rows = a.shape[1]

    def device(zz, xx, cc):
        return (zz, xx * 2 + cc)

    def along(o, sign=1):
        return ((x + sign * o[0] + 4) % 4) * 4 + (y + sign * o[1] + 4) % 4

    def remote(src, dst, send, recv, to):
        return pltpu.make_async_remote_copy(
            src_ref=src, dst_ref=dst, send_sem=send, recv_sem=recv, device_id=to, device_id_type=MESH
        )

    def half(ref, which, size):
        return ref.at[pl.ds(pl.multiple_of(which * size, size), size)]

    def load(i):
        return pltpu.make_async_copy(archive_hbm.at[pl.ds(i * rows, rows), :], a.at[i], a_sem.at[i])

    def save(i):
        return pltpu.make_async_copy(s.at[i], s_hbm.at[pl.ds(i * rows, rows), :], s_sem.at[i])

    load_sketch = pltpu.make_async_copy(sketch_hbm, sk, sk_sem)
    load_sketch.start()
    for i in range(PARTS):
        load(i).start()

    barrier = pltpu.get_barrier_semaphore()
    for o in PLANE:
        pl.semaphore_signal(barrier, inc=1, device_id=device(z, along(o), core), device_id_type=MESH)
    for o in LINE:
        for cc in range(2):
            pl.semaphore_signal(barrier, inc=1, device_id=device((z + o) % 8, xy, cc), device_id_type=MESH)
    sibling = device(z, xy, other)
    pl.semaphore_signal(barrier, inc=1, device_id=sibling, device_id_type=MESH)

    load_sketch.wait()
    for i in range(PARTS):
        load(i).wait()
        block = dot(a[i], sk[...])
        s[i] = block
        save(i).start()
        high, middle, _ = pieces(block.T)
        hm[i, :256] = high
        hm[i, 256:] = middle
    both = jnp.concatenate([hm[i] for i in range(PARTS)], axis=1)
    high, middle = both[:256], both[256:]
    first = dot_nt(both, high)
    mixed = first[256:]
    g[...] = ((first[:256] + dot_nt(middle, middle)) + (mixed + mixed.T)).reshape(32, 8, 256)

    def cross(which):
        columns = pl.ds(pl.multiple_of(which * 512, 512), 512)
        both = dot(hm[0], a[0, :, columns])
        for i in range(1, PARTS):
            both += dot(hm[i], a[i, :, columns])
        half(w, which, 64)[...] = (both[:256] + both[256:]).T.reshape(64, 8, 256)

    pl.semaphore_wait(barrier, 30)
    one = remote(half(g, other, 16), gcore, send1, recv1, sibling)
    one.start()
    one.wait()
    gcore[...] += half(g, core, 16)[...]

    def two(i):
        to = along(PLANE[i])
        return remote(gcore.at[to], gxy.at[i], send2.at[i], recv2.at[i], device(z, to, core))

    for i in range(15):
        two(i).start()
    cross(other)
    wone = remote(half(w, other, 64), wcore, wsend1, wrecv1, sibling)
    wone.start()
    cross(core)
    total = gcore[xy]
    for i in reversed(range(15)):
        two(i).wait_recv()
        total += gxy[i]
    gz[z] = total

    def three(i):
        return remote(gz.at[z], gz.at[z], send3.at[i], recv3.at[i], device((z + LINE[i]) % 8, xy, core))

    def three_in(i):
        slot = (z - LINE[i] + 8) % 8
        return remote(gz.at[slot], gz.at[slot], send3.at[i], recv3.at[i], device(slot, xy, core))

    for i in range(7):
        three(i).start()

    wone.wait()
    for t in range(4):
        for i in range(16):
            wtile[i, t] = wcore[t * 16 + i] + w[core * 64 + t * 16 + i]

    def wtwo(i):
        to = along(PLANE[i])
        return remote(wtile.at[to], wxy.at[i], wsend2.at[i], wrecv2.at[i], device(z, to, core))

    for i in range(15):
        wtwo(i).start()

    for i in reversed(range(7)):
        three_in(i).wait_recv()
    total = gz[0]
    for o in range(1, 8):
        total += gz[o]
    mine = core * 16 + xy
    gsum[mine] = total

    def four(i):
        return remote(gsum.at[mine], gsum.at[mine], send4.at[i], recv4.at[i], device(z, along(PLANE[i]), core))

    def four_in(i):
        slot = along(PLANE[i], -1)
        there = gsum.at[core * 16 + slot]
        return remote(there, there, send4.at[i], recv4.at[i], device(z, slot, core))

    for i in range(15):
        four(i).start()
    for i in reversed(range(15)):
        four_in(i).wait_recv()
    five = remote(half(gsum, core, 16), half(gsum, core, 16), send5, recv5, sibling)
    five_in = remote(half(gsum, other, 16), half(gsum, other, 16), send5, recv5, sibling)
    five.start()
    above = lax.broadcasted_iota(jnp.int32, (256, 256), 1) - lax.broadcasted_iota(jnp.int32, (256, 256), 0)
    m[:, 256:] = jnp.where(above == 0, 1.0, 0.0)
    five_in.wait_recv()
    m[:, :256] = gsum[...].reshape(256, 256)

    def wthree(t, cc):
        return remote(
            wsum.at[t], wz.at[z], wsend3.at[t * 2 + cc], wrecv3.at[z], device(core * 4 + t, xy, cc)
        )

    def here(t, cc):
        return jnp.logical_and(z == core * 4 + t, core == cc)

    def along_z():
        total = wtile[xy]
        for i in reversed(range(15)):
            wtwo(i).wait_recv()
            total += wxy[i]
        wsum[...] = total
        for t in range(4):
            for cc in range(2):

                @pl.when(jnp.logical_not(here(t, cc)))
                def _():
                    wthree(t, cc).start()

                @pl.when(here(t, cc))
                def _():
                    wz[z] = wsum[t]

    for top in range(0, 256, 64):
        factor(m, top)
        if top == 64:
            along_z()

    inverse = jnp.where(above <= 0, m[:, 256:], 0.0)
    high, middle, _ = pieces(inverse * root)
    inverse_ref[:, :256] = high
    inverse_ref[:, 256:] = middle
    r_ref[...] = jnp.where(above >= 0, m[:, :256] / root, 0.0)

    owner = z // 4
    for zz in range(8):

        @pl.when(jnp.logical_not(jnp.logical_and(z == zz, core == owner)))
        def _():
            remote(
                wsum.at[0], wz.at[zz], wsend3.at[0], wrecv3.at[zz], device(zz, xy, owner)
            ).wait_recv()

    total = wz[0]
    for zz in range(1, 8):
        total += wz[zz]
    p_ref[...] = lax.dot_general(
        jnp.where(core == 0, total[:4], total[4:]), inverse, NT,
        precision=lax.Precision.HIGHEST, preferred_element_type=F32,
    )

    for i in range(15):
        two(i).wait_send()
        four(i).wait_send()
        wtwo(i).wait_send()
    for i in range(7):
        three(i).wait_send()
    five.wait_send()
    for t in range(4):
        for cc in range(2):

            @pl.when(jnp.logical_not(here(t, cc)))
            def _():
                wthree(t, cc).wait_send()

    for i in range(PARTS):
        save(i).wait()


def row(tile, j):
    return jnp.broadcast_to(tile[j : j + 1, :], (8, 128))


def column(tile, k):
    return jnp.broadcast_to(tile[:, k : k + 1], (8, 128))


def factor(m, top):
    sublane = lax.broadcasted_iota(jnp.int32, (8, 128), 0)
    tiles = [0, 1, 2] if top < 128 else [1, 2, 3]
    at = tiles.index(top // 128)

    def place(g, t):
        return slice(top + 8 * g, top + 8 * g + 8), slice(128 * t, 128 * t + 128)

    r = [[m[place(g, t)] for t in tiles] for g in range(8)]
    for s in range(8):
        lane = (top + 8 * s) % 128
        c = {(g, k): column(r[g][at], lane + k) for g in range(s, 8) for k in range(8)}
        scale = jnp.zeros((8, 128), F32)
        for j in range(8):
            pivot = row(c[s, j], j)
            inverse = 1.0 / pivot
            scale = jnp.where(sublane == j, lax.rsqrt(pivot), scale)
            for g in range(s, 8):
                c[g, j] = c[g, j] * inverse
            below = jnp.where(sublane > j, c[s, j], 0.0)
            for k in range(j + 1, 8):
                across = row(c[s, k], j)
                for g in range(s, 8):
                    c[g, k] = c[g, k] - c[g, j] * across
            for t in range(3):
                across = row(r[s][t], j)
                r[s][t] = r[s][t] - below * across
                for g in range(s + 1, 8):
                    r[g][t] = r[g][t] - c[g, j] * across
        for t in range(3):
            r[s][t] = r[s][t] * scale
    for g in range(8):
        for i, t in enumerate(tiles):
            m[place(g, t)] = r[g][i]
    low = top + 64
    if low < 256:
        width = slice(128 * tiles[0], 128 * tiles[0] + 384)
        hl, ml, ll = pieces(m[top:low, low // 128 * 128 : 256])
        hp, mp, lp = pieces(m[top:low, width])
        update = lax.dot_general(
            jnp.concatenate([hl, hl, ml, ml], axis=0),
            jnp.concatenate([hp, mp, hp, mp], axis=0),
            TN, preferred_element_type=F32,
        )
        update += lax.dot_general(
            jnp.concatenate([hl, ll], axis=0), jnp.concatenate([lp, hp], axis=0), TN, preferred_element_type=F32
        )
        m[low:, width] -= update[low % 128 :]


def finish(inverse_ref, s_hbm, r_hbm, p_hbm, q_hbm, r_out, p_out, s, q, s_sem, q_sem, rp_sem):
    rows = s.shape[1]

    def load(i):
        return pltpu.make_async_copy(s_hbm.at[pl.ds(i * rows, rows), :], s.at[i], s_sem.at[i])

    def save(i):
        return pltpu.make_async_copy(q.at[i], q_hbm.at[pl.ds(i * rows, rows), :], q_sem.at[i])

    for i in range(CHUNKS):
        load(i).start()
    pass_r = pltpu.make_async_copy(r_hbm, r_out, rp_sem.at[0])
    pass_p = pltpu.make_async_copy(p_hbm, p_out, rp_sem.at[1])
    pass_r.start()
    pass_p.start()
    both = inverse_ref[...]
    both = jnp.concatenate([both, both[:, :256]], axis=1)
    for i in range(CHUNKS):
        load(i).wait()
        high, middle, _ = pieces(s[i])
        q[i] = dot_nt(jnp.concatenate([high, high, middle], axis=1), both).astype(BF16)
        save(i).start()
    for i in range(CHUNKS):
        save(i).wait()
    pass_r.wait()
    pass_p.wait()


def local(archive, sketch):
    pixels, depth = archive.shape
    rank = sketch.shape[1]
    rows = pixels // PARTS
    root = float(pixels * lax.axis_size("gx") * lax.axis_size("gy")) ** 0.5
    any_spec = pl.BlockSpec(memory_space=pl.ANY)
    vmem = pl.BlockSpec(memory_space=pltpu.VMEM)
    dma = pltpu.SemaphoreType.DMA
    s, inverse, r_factor, projection = pl.pallas_call(
        functools.partial(exchange, root),
        out_shape=(
            jax.ShapeDtypeStruct((pixels, rank), F32),
            jax.ShapeDtypeStruct((rank, 2 * rank), BF16),
            jax.ShapeDtypeStruct((rank, rank), F32),
            jax.ShapeDtypeStruct((4, rank), F32),
        ),
        in_specs=[any_spec, any_spec],
        out_specs=(any_spec, vmem, vmem, vmem),
        scratch_shapes=[
            pltpu.VMEM((PARTS, rows, depth), BF16),
            pltpu.VMEM((depth, rank), BF16),
            pltpu.VMEM((PARTS, rows, rank), F32),
            pltpu.VMEM((PARTS, 512, rows), BF16),
            pltpu.VMEM((32, 8, 256), F32),
            pltpu.VMEM((16, 8, 256), F32),
            pltpu.VMEM((15, 8, 256), F32),
            pltpu.VMEM((8, 8, 256), F32),
            pltpu.VMEM((32, 8, 256), F32),
            pltpu.VMEM((128, 8, 256), F32),
            pltpu.VMEM((64, 8, 256), F32),
            pltpu.VMEM((16, 4, 8, 256), F32),
            pltpu.VMEM((15, 4, 8, 256), F32),
            pltpu.VMEM((4, 8, 256), F32),
            pltpu.VMEM((8, 8, 256), F32),
            pltpu.VMEM((rank, 2 * rank), F32),
            dma((PARTS,)), dma((PARTS,)), dma, dma, dma, dma((15,)), dma((15,)),
            dma((7,)), dma((7,)), dma((15,)), dma((15,)), dma, dma,
            dma, dma, dma((15,)), dma((15,)), dma((8,)), dma((8,)),
        ],
        compiler_params=pltpu.CompilerParams(
            collective_id=0, has_side_effects=True, vmem_limit_bytes=60 * 2**20
        ),
    )(archive, sketch)
    chunk = pixels // CHUNKS
    return pl.pallas_call(
        finish,
        out_shape=(
            jax.ShapeDtypeStruct((pixels, rank), BF16),
            jax.ShapeDtypeStruct((rank, rank), F32),
            jax.ShapeDtypeStruct((4, rank), F32),
        ),
        in_specs=[vmem, any_spec, any_spec, any_spec],
        out_specs=(any_spec, any_spec, any_spec),
        scratch_shapes=[
            pltpu.VMEM((CHUNKS, chunk, rank), F32),
            pltpu.VMEM((CHUNKS, chunk, rank), BF16),
            dma((CHUNKS,)), dma((CHUNKS,)), dma((2,)),
        ],
        compiler_params=pltpu.CompilerParams(vmem_limit_bytes=60 * 2**20),
    )(inverse, s, r_factor, projection)


def solution(mesh):
    return jax.shard_map(
        local,
        mesh=mesh,
        in_specs=(P(("gx", "gy"), None), P()),
        out_specs=(P(("gx", "gy"), None), P(), P(("gx", "gy"), None)),
        check_vma=False,
    )
```

```python
import functools

import jax
import jax.numpy as jnp
from jax import lax
from jax.experimental import pallas as pl
from jax.experimental.pallas import tpu as pltpu
from jax.sharding import PartitionSpec as P

F32, BF16 = jnp.float32, jnp.bfloat16
PARTS = 2
CHUNKS = 4
MESH = pl.DeviceIdType.MESH
NT = (((1,), (1,)), ((), ()))
TN = (((0,), (0,)), ((), ()))


def dot(a, b):
    return jnp.dot(a, b, preferred_element_type=F32)


def dot_nt(a, b):
    return lax.dot_general(a, b, NT, preferred_element_type=F32)


def pieces(value):
    high = value.astype(BF16)
    rest = value - high.astype(F32)
    middle = rest.astype(BF16)
    return high, middle, (rest - middle.astype(F32)).astype(BF16)


PLANE = sorted(((i // 4, i % 4) for i in range(1, 16)), key=lambda o: -min(o[0], 4 - o[0]) - min(o[1], 4 - o[1]))
LINE = sorted(range(1, 8), key=lambda o: -min(o, 8 - o))


def exchange(
    root, archive_hbm, sketch_hbm, q_hbm, r_ref, p_ref,
    a, sk, s, hm, q, g, gcore, gxy, gz, gsum, w, wcore, wtile, wxy, wsum, wz, m,
    a_sem, q_sem, sk_sem, send1, recv1, send2, recv2, send3, recv3, send4, recv4,
    send5, recv5, wsend1, wrecv1, wsend2, wrecv2, wsend3, wrecv3,
):
    z, gy = lax.axis_index("gx"), lax.axis_index("gy")
    core, xy = gy % 2, gy // 2
    x, y = xy // 4, xy % 4
    other = 1 - core
    rows, chunk = a.shape[1], q.shape[1]

    def device(zz, xx, cc):
        return (zz, xx * 2 + cc)

    def along(o, sign=1):
        return ((x + sign * o[0] + 4) % 4) * 4 + (y + sign * o[1] + 4) % 4

    def remote(src, dst, send, recv, to):
        return pltpu.make_async_remote_copy(
            src_ref=src, dst_ref=dst, send_sem=send, recv_sem=recv, device_id=to, device_id_type=MESH
        )

    def half(ref, which, size):
        return ref.at[pl.ds(pl.multiple_of(which * size, size), size)]

    def load(i):
        return pltpu.make_async_copy(archive_hbm.at[pl.ds(i * rows, rows), :], a.at[i], a_sem.at[i])

    def save(i):
        return pltpu.make_async_copy(q.at[i], q_hbm.at[pl.ds(i * chunk, chunk), :], q_sem.at[i])

    load_sketch = pltpu.make_async_copy(sketch_hbm, sk, sk_sem)
    load_sketch.start()
    for i in range(PARTS):
        load(i).start()

    barrier = pltpu.get_barrier_semaphore()
    for o in PLANE:
        pl.semaphore_signal(barrier, inc=1, device_id=device(z, along(o), core), device_id_type=MESH)
    for o in LINE:
        for cc in range(2):
            pl.semaphore_signal(barrier, inc=1, device_id=device((z + o) % 8, xy, cc), device_id_type=MESH)
    sibling = device(z, xy, other)
    pl.semaphore_signal(barrier, inc=1, device_id=sibling, device_id_type=MESH)

    load_sketch.wait()
    for i in range(PARTS):
        load(i).wait()
        block = dot(a[i], sk[...])
        s[pl.ds(i * rows, rows)] = block
        high, middle, _ = pieces(block.T)
        hm[i, :256] = high
        hm[i, 256:] = middle
    both = jnp.concatenate([hm[i] for i in range(PARTS)], axis=1)
    high, middle = both[:256], both[256:]
    first = dot_nt(both, high)
    mixed = first[256:]
    g[...] = ((first[:256] + dot_nt(middle, middle)) + (mixed + mixed.T)).reshape(32, 8, 256)

    def cross(which):
        columns = pl.ds(pl.multiple_of(which * 512, 512), 512)
        both = dot(hm[0], a[0, :, columns])
        for i in range(1, PARTS):
            both += dot(hm[i], a[i, :, columns])
        half(w, which, 64)[...] = (both[:256] + both[256:]).T.reshape(64, 8, 256)

    pl.semaphore_wait(barrier, 30)
    one = remote(half(g, other, 16), gcore, send1, recv1, sibling)
    one.start()
    one.wait()
    gcore[...] += half(g, core, 16)[...]

    def two(i):
        to = along(PLANE[i])
        return remote(gcore.at[to], gxy.at[i], send2.at[i], recv2.at[i], device(z, to, core))

    for i in range(15):
        two(i).start()
    cross(other)
    wone = remote(half(w, other, 64), wcore, wsend1, wrecv1, sibling)
    wone.start()
    cross(core)
    total = gcore[xy]
    for i in reversed(range(15)):
        two(i).wait_recv()
        total += gxy[i]
    gz[z] = total

    def three(i):
        return remote(gz.at[z], gz.at[z], send3.at[i], recv3.at[i], device((z + LINE[i]) % 8, xy, core))

    def three_in(i):
        slot = (z - LINE[i] + 8) % 8
        return remote(gz.at[slot], gz.at[slot], send3.at[i], recv3.at[i], device(slot, xy, core))

    for i in range(7):
        three(i).start()

    wone.wait()
    for t in range(4):
        for i in range(16):
            wtile[i, t] = wcore[t * 16 + i] + w[core * 64 + t * 16 + i]

    def wtwo(i):
        to = along(PLANE[i])
        return remote(wtile.at[to], wxy.at[i], wsend2.at[i], wrecv2.at[i], device(z, to, core))

    for i in range(15):
        wtwo(i).start()

    for i in reversed(range(7)):
        three_in(i).wait_recv()
    total = gz[0]
    for o in range(1, 8):
        total += gz[o]
    mine = core * 16 + xy
    gsum[mine] = total

    def four(i):
        return remote(gsum.at[mine], gsum.at[mine], send4.at[i], recv4.at[i], device(z, along(PLANE[i]), core))

    def four_in(i):
        slot = along(PLANE[i], -1)
        there = gsum.at[core * 16 + slot]
        return remote(there, there, send4.at[i], recv4.at[i], device(z, slot, core))

    for i in range(15):
        four(i).start()
    for i in reversed(range(15)):
        four_in(i).wait_recv()
    five = remote(half(gsum, core, 16), half(gsum, core, 16), send5, recv5, sibling)
    five_in = remote(half(gsum, other, 16), half(gsum, other, 16), send5, recv5, sibling)
    five.start()
    above = lax.broadcasted_iota(jnp.int32, (256, 256), 1) - lax.broadcasted_iota(jnp.int32, (256, 256), 0)
    m[:, 256:] = jnp.where(above == 0, 1.0, 0.0)

    def wthree(t, cc):
        return remote(
            wsum.at[t], wz.at[z], wsend3.at[t * 2 + cc], wrecv3.at[z], device(core * 4 + t, xy, cc)
        )

    def here(t, cc):
        return jnp.logical_and(z == core * 4 + t, core == cc)

    def along_z():
        total = wtile[xy]
        for i in reversed(range(15)):
            wtwo(i).wait_recv()
            total += wxy[i]
        wsum[...] = total
        for t in range(4):
            for cc in range(2):

                @pl.when(jnp.logical_not(here(t, cc)))
                def _():
                    wthree(t, cc).start()

                @pl.when(here(t, cc))
                def _():
                    wz[z] = wsum[t]

    along_z()
    five_in.wait_recv()
    m[:, :256] = gsum[...].reshape(256, 256)
    for top in range(0, 256, 64):
        factor(m, top)

    inverse = jnp.where(above <= 0, m[:, 256:], 0.0)
    high, middle, _ = pieces(inverse * root)
    scaled = jnp.concatenate([high, middle, high], axis=1)
    for i in range(CHUNKS):
        high, middle, _ = pieces(s[pl.ds(i * chunk, chunk)])
        q[i] = dot_nt(jnp.concatenate([high, high, middle], axis=1), scaled).astype(BF16)
        save(i).start()
    r_ref[...] = jnp.where(above >= 0, m[:, :256] / root, 0.0)

    owner = z // 4
    for zz in range(8):

        @pl.when(jnp.logical_not(jnp.logical_and(z == zz, core == owner)))
        def _():
            remote(
                wsum.at[0], wz.at[zz], wsend3.at[0], wrecv3.at[zz], device(zz, xy, owner)
            ).wait_recv()

    total = wz[0]
    for zz in range(1, 8):
        total += wz[zz]
    p_ref[...] = lax.dot_general(
        jnp.where(core == 0, total[:4], total[4:]), inverse, NT,
        precision=lax.Precision.HIGHEST, preferred_element_type=F32,
    )

    for i in range(15):
        two(i).wait_send()
        four(i).wait_send()
        wtwo(i).wait_send()
    for i in range(7):
        three(i).wait_send()
    five.wait_send()
    for t in range(4):
        for cc in range(2):

            @pl.when(jnp.logical_not(here(t, cc)))
            def _():
                wthree(t, cc).wait_send()

    for i in range(CHUNKS):
        save(i).wait()


def row(tile, j):
    return jnp.broadcast_to(tile[j : j + 1, :], (8, 128))


def column(tile, k):
    return jnp.broadcast_to(tile[:, k : k + 1], (8, 128))


def factor(m, top):
    sublane = lax.broadcasted_iota(jnp.int32, (8, 128), 0)
    tiles = [0, 1, 2] if top < 128 else [1, 2, 3]
    at = tiles.index(top // 128)

    def place(g, t):
        return slice(top + 8 * g, top + 8 * g + 8), slice(128 * t, 128 * t + 128)

    r = [[m[place(g, t)] for t in tiles] for g in range(8)]
    ahead = [column(r[0][at], top % 128 + k) for k in range(8)]
    for s in range(8):
        lane = (top + 8 * s) % 128
        c = {(g, k): column(r[g][at], lane + k) for g in range(s + 1, 8) for k in range(8)}
        for k in range(8):
            c[s, k] = ahead[k]
        ahead = [column(r[s + 1][at], lane + 8 + k) for k in range(8)] if s < 7 else []
        scale = jnp.zeros((8, 128), F32)
        for j in range(8):
            pivot = row(c[s, j], j)
            inverse = 1.0 / pivot
            scale = jnp.where(sublane == j, lax.rsqrt(pivot), scale)
            across = [row(c[s + 1, j], k) for k in range(len(ahead))]
            for g in range(s, 8):
                c[g, j] = c[g, j] * inverse
            for k in range(len(ahead)):
                ahead[k] = ahead[k] - c[s + 1, j] * across[k]
            below = jnp.where(sublane > j, c[s, j], 0.0)
            for k in range(j + 1, 8):
                across = row(c[s, k], j)
                for g in range(s, 8):
                    c[g, k] = c[g, k] - c[g, j] * across
            for t in range(3):
                across = row(r[s][t], j)
                r[s][t] = r[s][t] - below * across
                for g in range(s + 1, 8):
                    r[g][t] = r[g][t] - c[g, j] * across
        for t in range(3):
            r[s][t] = r[s][t] * scale
    for g in range(8):
        for i, t in enumerate(tiles):
            m[place(g, t)] = r[g][i]
    low = top + 64
    if low < 256:
        width = slice(128 * tiles[0], 128 * tiles[0] + 384)
        hl, ml, ll = pieces(m[top:low, low // 128 * 128 : 256])
        hp, mp, lp = pieces(m[top:low, width])
        update = lax.dot_general(
            jnp.concatenate([hl, hl, ml, ml], axis=0),
            jnp.concatenate([hp, mp, hp, mp], axis=0),
            TN, preferred_element_type=F32,
        )
        update += lax.dot_general(
            jnp.concatenate([hl, ll], axis=0), jnp.concatenate([lp, hp], axis=0), TN, preferred_element_type=F32
        )
        m[low:, width] -= update[low % 128 :]


def local(archive, sketch):
    pixels, depth = archive.shape
    rank = sketch.shape[1]
    rows = pixels // PARTS
    root = float(pixels * lax.axis_size("gx") * lax.axis_size("gy")) ** 0.5
    any_spec = pl.BlockSpec(memory_space=pl.ANY)
    vmem = pl.BlockSpec(memory_space=pltpu.VMEM)
    dma = pltpu.SemaphoreType.DMA
    return pl.pallas_call(
        functools.partial(exchange, root),
        out_shape=(
            jax.ShapeDtypeStruct((pixels, rank), BF16),
            jax.ShapeDtypeStruct((rank, rank), F32),
            jax.ShapeDtypeStruct((4, rank), F32),
        ),
        in_specs=[any_spec, any_spec],
        out_specs=(any_spec, vmem, vmem),
        scratch_shapes=[
            pltpu.VMEM((PARTS, rows, depth), BF16),
            pltpu.VMEM((depth, rank), BF16),
            pltpu.VMEM((pixels, rank), F32),
            pltpu.VMEM((PARTS, 512, rows), BF16),
            pltpu.VMEM((CHUNKS, pixels // CHUNKS, rank), BF16),
            pltpu.VMEM((32, 8, 256), F32),
            pltpu.VMEM((16, 8, 256), F32),
            pltpu.VMEM((15, 8, 256), F32),
            pltpu.VMEM((8, 8, 256), F32),
            pltpu.VMEM((32, 8, 256), F32),
            pltpu.VMEM((128, 8, 256), F32),
            pltpu.VMEM((64, 8, 256), F32),
            pltpu.VMEM((16, 4, 8, 256), F32),
            pltpu.VMEM((15, 4, 8, 256), F32),
            pltpu.VMEM((4, 8, 256), F32),
            pltpu.VMEM((8, 8, 256), F32),
            pltpu.VMEM((rank, 2 * rank), F32),
            dma((PARTS,)), dma((CHUNKS,)), dma, dma, dma, dma((15,)), dma((15,)),
            dma((7,)), dma((7,)), dma((15,)), dma((15,)), dma, dma,
            dma, dma, dma((15,)), dma((15,)), dma((8,)), dma((8,)),
        ],
        compiler_params=pltpu.CompilerParams(
            collective_id=0, has_side_effects=True, vmem_limit_bytes=60 * 2**20
        ),
    )(archive, sketch)


def solution(mesh):
    return jax.shard_map(
        local,
        mesh=mesh,
        in_specs=(P(("gx", "gy"), None), P()),
        out_specs=(P(("gx", "gy"), None), P(), P(("gx", "gy"), None)),
        check_vma=False,
    )
```

```python
import functools

import jax
import jax.numpy as jnp
from jax import lax
from jax.experimental import pallas as pl
from jax.experimental.pallas import tpu as pltpu
from jax.sharding import PartitionSpec as P

F32, BF16 = jnp.float32, jnp.bfloat16
PARTS = 2
CHUNKS = 4
MESH = pl.DeviceIdType.MESH
NT = (((1,), (1,)), ((), ()))
TN = (((0,), (0,)), ((), ()))


def dot(a, b):
    return jnp.dot(a, b, preferred_element_type=F32)


def dot_nt(a, b):
    return lax.dot_general(a, b, NT, preferred_element_type=F32)


def pieces(value):
    high = value.astype(BF16)
    rest = value - high.astype(F32)
    middle = rest.astype(BF16)
    return high, middle, (rest - middle.astype(F32)).astype(BF16)


PLANE = sorted(((i // 4, i % 4) for i in range(1, 16)), key=lambda o: -min(o[0], 4 - o[0]) - min(o[1], 4 - o[1]))
LINE = sorted(range(1, 8), key=lambda o: -min(o, 8 - o))


def exchange(
    root, archive_hbm, sketch_hbm, q_ref, r_ref, p_ref,
    a, sk, s, hm, g, gcore, gxy, gz, gsum, w, wcore, wtile, wxy, wsum, wz, m,
    a_sem, sk_sem, send1, recv1, send2, recv2, send3, recv3, send4, recv4,
    send5, recv5, wsend1, wrecv1, wsend2, wrecv2, wsend3, wrecv3,
):
    z, gy = lax.axis_index("gx"), lax.axis_index("gy")
    core, xy = gy % 2, gy // 2
    x, y = xy // 4, xy % 4
    other = 1 - core
    rows, chunk = a.shape[1], s.shape[0] // CHUNKS

    def device(zz, xx, cc):
        return (zz, xx * 2 + cc)

    def along(o, sign=1):
        return ((x + sign * o[0] + 4) % 4) * 4 + (y + sign * o[1] + 4) % 4

    def remote(src, dst, send, recv, to):
        return pltpu.make_async_remote_copy(
            src_ref=src, dst_ref=dst, send_sem=send, recv_sem=recv, device_id=to, device_id_type=MESH
        )

    def half(ref, which, size):
        return ref.at[pl.ds(pl.multiple_of(which * size, size), size)]

    def load(i):
        return pltpu.make_async_copy(archive_hbm.at[pl.ds(i * rows, rows), :], a.at[i], a_sem.at[i])

    load_sketch = pltpu.make_async_copy(sketch_hbm, sk, sk_sem)
    load_sketch.start()
    for i in range(PARTS):
        load(i).start()

    barrier = pltpu.get_barrier_semaphore()
    for o in PLANE:
        pl.semaphore_signal(barrier, inc=1, device_id=device(z, along(o), core), device_id_type=MESH)
    for o in LINE:
        for cc in range(2):
            pl.semaphore_signal(barrier, inc=1, device_id=device((z + o) % 8, xy, cc), device_id_type=MESH)
    sibling = device(z, xy, other)
    pl.semaphore_signal(barrier, inc=1, device_id=sibling, device_id_type=MESH)

    load_sketch.wait()
    for i in range(PARTS):
        load(i).wait()
        block = dot(a[i], sk[...])
        high, middle, _ = pieces(block)
        block = jnp.concatenate([high, middle], axis=1)
        s[pl.ds(i * rows, rows)] = block
        hm[i] = block.T
    both = jnp.concatenate([hm[i] for i in range(PARTS)], axis=1)
    high, middle = both[:256], both[256:]
    first = dot_nt(both, high)
    mixed = first[256:]
    g[...] = ((first[:256] + dot_nt(middle, middle)) + (mixed + mixed.T)).reshape(32, 8, 256)

    def cross(which):
        columns = pl.ds(pl.multiple_of(which * 512, 512), 512)
        both = dot(hm[0], a[0, :, columns])
        for i in range(1, PARTS):
            both += dot(hm[i], a[i, :, columns])
        half(w, which, 64)[...] = (both[:256] + both[256:]).T.reshape(64, 8, 256)

    pl.semaphore_wait(barrier, 30)
    one = remote(half(g, other, 16), gcore, send1, recv1, sibling)
    one.start()
    one.wait()
    gcore[...] += half(g, core, 16)[...]

    def two(i):
        to = along(PLANE[i])
        return remote(gcore.at[to], gxy.at[i], send2.at[i], recv2.at[i], device(z, to, core))

    for i in range(15):
        two(i).start()
    cross(other)
    wone = remote(half(w, other, 64), wcore, wsend1, wrecv1, sibling)
    wone.start()
    cross(core)
    total = gcore[xy]
    for i in reversed(range(15)):
        two(i).wait_recv()
        total += gxy[i]
    gz[z] = total

    def three(i):
        return remote(gz.at[z], gz.at[z], send3.at[i], recv3.at[i], device((z + LINE[i]) % 8, xy, core))

    def three_in(i):
        slot = (z - LINE[i] + 8) % 8
        return remote(gz.at[slot], gz.at[slot], send3.at[i], recv3.at[i], device(slot, xy, core))

    for i in range(7):
        three(i).start()

    wone.wait()
    for t in range(4):
        for i in range(16):
            wtile[i, t] = wcore[t * 16 + i] + w[core * 64 + t * 16 + i]

    def wtwo(i):
        to = along(PLANE[i])
        return remote(wtile.at[to], wxy.at[i], wsend2.at[i], wrecv2.at[i], device(z, to, core))

    for i in range(15):
        wtwo(i).start()

    for i in reversed(range(7)):
        three_in(i).wait_recv()
    total = gz[0]
    for o in range(1, 8):
        total += gz[o]
    mine = core * 16 + xy
    gsum[mine] = total

    def four(i):
        return remote(gsum.at[mine], gsum.at[mine], send4.at[i], recv4.at[i], device(z, along(PLANE[i]), core))

    def four_in(i):
        slot = along(PLANE[i], -1)
        there = gsum.at[core * 16 + slot]
        return remote(there, there, send4.at[i], recv4.at[i], device(z, slot, core))

    for i in range(15):
        four(i).start()
    for i in reversed(range(15)):
        four_in(i).wait_recv()
    five = remote(half(gsum, core, 16), half(gsum, core, 16), send5, recv5, sibling)
    five_in = remote(half(gsum, other, 16), half(gsum, other, 16), send5, recv5, sibling)
    five.start()
    above = lax.broadcasted_iota(jnp.int32, (256, 256), 1) - lax.broadcasted_iota(jnp.int32, (256, 256), 0)
    m[:, 256:] = jnp.where(above == 0, 1.0, 0.0)

    def wthree(t, cc):
        return remote(
            wsum.at[t], wz.at[z], wsend3.at[t * 2 + cc], wrecv3.at[z], device(core * 4 + t, xy, cc)
        )

    def here(t, cc):
        return jnp.logical_and(z == core * 4 + t, core == cc)

    def along_z():
        total = wtile[xy]
        for i in reversed(range(15)):
            wtwo(i).wait_recv()
            total += wxy[i]
        wsum[...] = total
        for t in range(4):
            for cc in range(2):

                @pl.when(jnp.logical_not(here(t, cc)))
                def _():
                    wthree(t, cc).start()

                @pl.when(here(t, cc))
                def _():
                    wz[z] = wsum[t]

    along_z()
    five_in.wait_recv()
    m[:, :256] = gsum[...].reshape(256, 256)
    for top in range(0, 256, 64):
        factor(m, top)

    inverse = jnp.where(above <= 0, m[:, 256:], 0.0)
    high, middle, _ = pieces(inverse * root)
    scaled = jnp.concatenate([high, high, middle], axis=1)
    for i in range(CHUNKS):
        block = s[pl.ds(i * chunk, chunk)]
        q_ref[pl.ds(i * chunk, chunk)] = dot_nt(
            jnp.concatenate([block, block[:, :256]], axis=1), scaled
        ).astype(BF16)
    r_ref[...] = jnp.where(above >= 0, m[:, :256] / root, 0.0)

    owner = z // 4
    for zz in range(8):

        @pl.when(jnp.logical_not(jnp.logical_and(z == zz, core == owner)))
        def _():
            remote(
                wsum.at[0], wz.at[zz], wsend3.at[0], wrecv3.at[zz], device(zz, xy, owner)
            ).wait_recv()

    total = wz[0]
    for zz in range(1, 8):
        total += wz[zz]
    p_ref[...] = lax.dot_general(
        jnp.where(core == 0, total[:4], total[4:]), inverse, NT,
        precision=lax.Precision.HIGHEST, preferred_element_type=F32,
    )

    for i in range(15):
        two(i).wait_send()
        four(i).wait_send()
        wtwo(i).wait_send()
    for i in range(7):
        three(i).wait_send()
    five.wait_send()
    for t in range(4):
        for cc in range(2):

            @pl.when(jnp.logical_not(here(t, cc)))
            def _():
                wthree(t, cc).wait_send()


def row(tile, j):
    return jnp.broadcast_to(tile[j : j + 1, :], (8, 128))


def column(tile, k):
    return jnp.broadcast_to(tile[:, k : k + 1], (8, 128))


def factor(m, top):
    sublane = lax.broadcasted_iota(jnp.int32, (8, 128), 0)
    tiles = [0, 1, 2] if top < 128 else [1, 2, 3]
    at = tiles.index(top // 128)

    def place(g, t):
        return slice(top + 8 * g, top + 8 * g + 8), slice(128 * t, 128 * t + 128)

    r = [[m[place(g, t)] for t in tiles] for g in range(8)]
    ahead = [column(r[0][at], top % 128 + k) for k in range(8)]
    for s in range(8):
        lane = (top + 8 * s) % 128
        c = {(g, k): column(r[g][at], lane + k) for g in range(s + 1, 8) for k in range(8)}
        for k in range(8):
            c[s, k] = ahead[k]
        ahead = [column(r[s + 1][at], lane + 8 + k) for k in range(8)] if s < 7 else []
        scale = jnp.zeros((8, 128), F32)
        for j in range(8):
            pivot = row(c[s, j], j)
            inverse = 1.0 / pivot
            scale = jnp.where(sublane == j, lax.rsqrt(pivot), scale)
            across = [row(c[s + 1, j], k) for k in range(len(ahead))]
            for g in range(s, 8):
                c[g, j] = c[g, j] * inverse
            for k in range(len(ahead)):
                ahead[k] = ahead[k] - c[s + 1, j] * across[k]
            below = jnp.where(sublane > j, c[s, j], 0.0)
            for k in range(j + 1, 8):
                across = row(c[s, k], j)
                for g in range(s, 8):
                    c[g, k] = c[g, k] - c[g, j] * across
            for t in range(3):
                across = row(r[s][t], j)
                r[s][t] = r[s][t] - below * across
                for g in range(s + 1, 8):
                    r[g][t] = r[g][t] - c[g, j] * across
        for t in range(3):
            r[s][t] = r[s][t] * scale
    for g in range(8):
        for i, t in enumerate(tiles):
            m[place(g, t)] = r[g][i]
    low = top + 64
    if low < 256:
        width = slice(128 * tiles[0], 128 * tiles[0] + 384)
        hl, ml, ll = pieces(m[top:low, low // 128 * 128 : 256])
        hp, mp, lp = pieces(m[top:low, width])
        update = lax.dot_general(
            jnp.concatenate([hl, hl, ml, ml], axis=0),
            jnp.concatenate([hp, mp, hp, mp], axis=0),
            TN, preferred_element_type=F32,
        )
        update += lax.dot_general(
            jnp.concatenate([hl, ll], axis=0), jnp.concatenate([lp, hp], axis=0), TN, preferred_element_type=F32
        )
        m[low:, width] -= update[low % 128 :]


def deliver(q, r, p, q_hbm, r_hbm, p_hbm, sem):
    copies = [
        pltpu.make_async_copy(src, dst, sem.at[i])
        for i, (src, dst) in enumerate([(q, q_hbm), (r, r_hbm), (p, p_hbm)])
    ]
    for copy in copies:
        copy.start()
    for copy in copies:
        copy.wait()


def local(archive, sketch):
    pixels, depth = archive.shape
    rank = sketch.shape[1]
    rows = pixels // PARTS
    root = float(pixels * lax.axis_size("gx") * lax.axis_size("gy")) ** 0.5
    any_spec = pl.BlockSpec(memory_space=pl.ANY)
    vmem = pl.BlockSpec(memory_space=pltpu.VMEM)
    dma = pltpu.SemaphoreType.DMA
    results = pl.pallas_call(
        functools.partial(exchange, root),
        out_shape=(
            pltpu.VMEM((pixels, rank), BF16),
            pltpu.VMEM((rank, rank), F32),
            pltpu.VMEM((4, rank), F32),
        ),
        in_specs=[any_spec, any_spec],
        out_specs=(vmem, vmem, vmem),
        scratch_shapes=[
            pltpu.VMEM((PARTS, rows, depth), BF16),
            pltpu.VMEM((depth, rank), BF16),
            pltpu.VMEM((pixels, 2 * rank), BF16),
            pltpu.VMEM((PARTS, 512, rows), BF16),
            pltpu.VMEM((32, 8, 256), F32),
            pltpu.VMEM((16, 8, 256), F32),
            pltpu.VMEM((15, 8, 256), F32),
            pltpu.VMEM((8, 8, 256), F32),
            pltpu.VMEM((32, 8, 256), F32),
            pltpu.VMEM((128, 8, 256), F32),
            pltpu.VMEM((64, 8, 256), F32),
            pltpu.VMEM((16, 4, 8, 256), F32),
            pltpu.VMEM((15, 4, 8, 256), F32),
            pltpu.VMEM((4, 8, 256), F32),
            pltpu.VMEM((8, 8, 256), F32),
            pltpu.VMEM((rank, 2 * rank), F32),
            dma((PARTS,)), dma, dma, dma, dma((15,)), dma((15,)),
            dma((7,)), dma((7,)), dma((15,)), dma((15,)), dma, dma,
            dma, dma, dma((15,)), dma((15,)), dma((8,)), dma((8,)),
        ],
        compiler_params=pltpu.CompilerParams(
            collective_id=0, has_side_effects=True, vmem_limit_bytes=52 * 2**20
        ),
    )(archive, sketch)
    return pl.pallas_call(
        deliver,
        out_shape=tuple(jax.ShapeDtypeStruct(r.shape, r.dtype) for r in results),
        in_specs=[vmem] * 3,
        out_specs=(any_spec,) * 3,
        scratch_shapes=[dma((3,))],
        compiler_params=pltpu.CompilerParams(vmem_limit_bytes=4 * 2**20),
    )(*results)


def solution(mesh):
    return jax.shard_map(
        local,
        mesh=mesh,
        in_specs=(P(("gx", "gy"), None), P()),
        out_specs=(P(("gx", "gy"), None), P(), P(("gx", "gy"), None)),
        check_vma=False,
    )
```

```python
import functools

import jax
import jax.numpy as jnp
from jax import lax
from jax.experimental import pallas as pl
from jax.experimental.pallas import tpu as pltpu
from jax.sharding import PartitionSpec as P

F32, BF16 = jnp.float32, jnp.bfloat16
SPLIT = (0, 3072, 4096)
CHUNKS = 4
MESH = pl.DeviceIdType.MESH
NT = (((1,), (1,)), ((), ()))
TN = (((0,), (0,)), ((), ()))


def dot(a, b):
    return jnp.dot(a, b, preferred_element_type=F32)


def dot_nt(a, b):
    return lax.dot_general(a, b, NT, preferred_element_type=F32)


def pieces(value):
    high = value.astype(BF16)
    rest = value - high.astype(F32)
    middle = rest.astype(BF16)
    return high, middle, (rest - middle.astype(F32)).astype(BF16)


PLANE = sorted(((i // 4, i % 4) for i in range(1, 16)), key=lambda o: -min(o[0], 4 - o[0]) - min(o[1], 4 - o[1]))
LINE = sorted(range(1, 8), key=lambda o: -min(o, 8 - o))


def exchange(
    root, archive_hbm, sketch_hbm, q_ref, r_ref, p_ref,
    a, sk, s, hm, g, gcore, gxy, gz, gsum, w, wcore, wtile, wxy, wsum, wz, m,
    a_sem, sk_sem, send1, recv1, send2, recv2, send3, recv3, send4, recv4,
    send5, recv5, wsend1, wrecv1, wsend2, wrecv2, wsend3, wrecv3,
):
    z, gy = lax.axis_index("gx"), lax.axis_index("gy")
    core, xy = gy % 2, gy // 2
    x, y = xy // 4, xy % 4
    other = 1 - core
    chunk = s.shape[0] // CHUNKS
    parts = [slice(i, j) for i, j in zip(SPLIT, SPLIT[1:])]

    def device(zz, xx, cc):
        return (zz, xx * 2 + cc)

    def along(o, sign=1):
        return ((x + sign * o[0] + 4) % 4) * 4 + (y + sign * o[1] + 4) % 4

    def remote(src, dst, send, recv, to):
        return pltpu.make_async_remote_copy(
            src_ref=src, dst_ref=dst, send_sem=send, recv_sem=recv, device_id=to, device_id_type=MESH
        )

    def half(ref, which, size):
        return ref.at[pl.ds(pl.multiple_of(which * size, size), size)]

    def load(i):
        return pltpu.make_async_copy(archive_hbm.at[parts[i]], a.at[parts[i]], a_sem.at[i])

    load_sketch = pltpu.make_async_copy(sketch_hbm, sk, sk_sem)
    load_sketch.start()
    for i in range(len(parts)):
        load(i).start()

    barrier = pltpu.get_barrier_semaphore()
    for o in PLANE:
        pl.semaphore_signal(barrier, inc=1, device_id=device(z, along(o), core), device_id_type=MESH)
    for o in LINE:
        for cc in range(2):
            pl.semaphore_signal(barrier, inc=1, device_id=device((z + o) % 8, xy, cc), device_id_type=MESH)
    sibling = device(z, xy, other)
    pl.semaphore_signal(barrier, inc=1, device_id=sibling, device_id_type=MESH)

    load_sketch.wait()
    for i, part in enumerate(parts):
        load(i).wait()
        high, middle, _ = pieces(dot(a[part], sk[...]))
        block = jnp.concatenate([high, middle], axis=1)
        s[part] = block
        hm[:, part] = block.T

    def gram(which):
        first = pl.multiple_of(which * 128, 128)
        mine = jnp.concatenate([hm[pl.ds(first, 128)], hm[pl.ds(first + 256, 128)]], axis=0)
        four = dot_nt(mine, hm[...])
        four = four[:, :256] + four[:, 256:]
        half(g, which, 16)[...] = (four[:128] + four[128:]).reshape(16, 8, 256)

    def cross(which):
        columns = pl.ds(pl.multiple_of(which * 512, 512), 512)
        both = dot(hm[...], a[:, columns])
        half(w, which, 64)[...] = (both[:256] + both[256:]).T.reshape(64, 8, 256)

    gram(other)
    pl.semaphore_wait(barrier, 30)
    one = remote(half(g, other, 16), gcore, send1, recv1, sibling)
    one.start()
    gram(core)
    one.wait()
    gcore[...] += half(g, core, 16)[...]

    def two(i):
        to = along(PLANE[i])
        return remote(gcore.at[to], gxy.at[i], send2.at[i], recv2.at[i], device(z, to, core))

    for i in range(15):
        two(i).start()
    cross(other)
    wone = remote(half(w, other, 64), wcore, wsend1, wrecv1, sibling)
    wone.start()
    cross(core)
    total = gcore[xy]
    for i in reversed(range(15)):
        two(i).wait_recv()
        total += gxy[i]
    gz[z] = total

    def three(i):
        return remote(gz.at[z], gz.at[z], send3.at[i], recv3.at[i], device((z + LINE[i]) % 8, xy, core))

    def three_in(i):
        slot = (z - LINE[i] + 8) % 8
        return remote(gz.at[slot], gz.at[slot], send3.at[i], recv3.at[i], device(slot, xy, core))

    for i in range(7):
        three(i).start()

    wone.wait()
    for t in range(4):
        for i in range(16):
            wtile[i, t] = wcore[t * 16 + i] + w[core * 64 + t * 16 + i]

    def wtwo(i):
        to = along(PLANE[i])
        return remote(wtile.at[to], wxy.at[i], wsend2.at[i], wrecv2.at[i], device(z, to, core))

    for i in range(15):
        wtwo(i).start()

    for i in reversed(range(7)):
        three_in(i).wait_recv()
    total = gz[0]
    for o in range(1, 8):
        total += gz[o]
    mine = core * 16 + xy
    gsum[mine] = total

    def four(i):
        return remote(gsum.at[mine], gsum.at[mine], send4.at[i], recv4.at[i], device(z, along(PLANE[i]), core))

    def four_in(i):
        slot = along(PLANE[i], -1)
        there = gsum.at[core * 16 + slot]
        return remote(there, there, send4.at[i], recv4.at[i], device(z, slot, core))

    for i in range(15):
        four(i).start()
    for i in reversed(range(15)):
        four_in(i).wait_recv()
    five = remote(half(gsum, core, 16), half(gsum, core, 16), send5, recv5, sibling)
    five_in = remote(half(gsum, other, 16), half(gsum, other, 16), send5, recv5, sibling)
    five.start()
    above = lax.broadcasted_iota(jnp.int32, (256, 256), 1) - lax.broadcasted_iota(jnp.int32, (256, 256), 0)
    m[:, 256:] = jnp.where(above == 0, 1.0, 0.0)

    def wthree(t, cc):
        return remote(
            wsum.at[t], wz.at[z], wsend3.at[t * 2 + cc], wrecv3.at[z], device(core * 4 + t, xy, cc)
        )

    def here(t, cc):
        return jnp.logical_and(z == core * 4 + t, core == cc)

    def along_z():
        total = wtile[xy]
        for i in reversed(range(15)):
            wtwo(i).wait_recv()
            total += wxy[i]
        wsum[...] = total
        for t in range(4):
            for cc in range(2):

                @pl.when(jnp.logical_not(here(t, cc)))
                def _():
                    wthree(t, cc).start()

                @pl.when(here(t, cc))
                def _():
                    wz[z] = wsum[t]

    along_z()
    five_in.wait_recv()
    m[:, :256] = gsum[...].reshape(256, 256)
    for top in range(0, 256, 64):
        factor(m, top)

    inverse = jnp.where(above <= 0, m[:, 256:], 0.0)
    high, middle, _ = pieces(inverse * root)
    scaled = jnp.concatenate([high, high, middle], axis=1)
    for i in range(CHUNKS):
        block = s[pl.ds(i * chunk, chunk)]
        q_ref[pl.ds(i * chunk, chunk)] = dot_nt(
            jnp.concatenate([block, block[:, :256]], axis=1), scaled
        ).astype(BF16)
    r_ref[...] = jnp.where(above >= 0, m[:, :256] / root, 0.0)

    owner = z // 4
    for zz in range(8):

        @pl.when(jnp.logical_not(jnp.logical_and(z == zz, core == owner)))
        def _():
            remote(
                wsum.at[0], wz.at[zz], wsend3.at[0], wrecv3.at[zz], device(zz, xy, owner)
            ).wait_recv()

    total = wz[0]
    for zz in range(1, 8):
        total += wz[zz]
    p_ref[...] = lax.dot_general(
        jnp.where(core == 0, total[:4], total[4:]), inverse, NT,
        precision=lax.Precision.HIGHEST, preferred_element_type=F32,
    )

    for i in range(15):
        two(i).wait_send()
        four(i).wait_send()
        wtwo(i).wait_send()
    for i in range(7):
        three(i).wait_send()
    five.wait_send()
    for t in range(4):
        for cc in range(2):

            @pl.when(jnp.logical_not(here(t, cc)))
            def _():
                wthree(t, cc).wait_send()


def row(tile, j):
    return jnp.broadcast_to(tile[j : j + 1, :], (8, 128))


def column(tile, k):
    return jnp.broadcast_to(tile[:, k : k + 1], (8, 128))


def factor(m, top):
    sublane = lax.broadcasted_iota(jnp.int32, (8, 128), 0)
    tiles = [0, 1, 2] if top < 128 else [1, 2, 3]
    at = tiles.index(top // 128)

    def place(g, t):
        return slice(top + 8 * g, top + 8 * g + 8), slice(128 * t, 128 * t + 128)

    r = [[m[place(g, t)] for t in tiles] for g in range(8)]
    ahead = [column(r[0][at], top % 128 + k) for k in range(8)]
    for s in range(8):
        lane = (top + 8 * s) % 128
        c = {(g, k): column(r[g][at], lane + k) for g in range(s + 1, 8) for k in range(8)}
        for k in range(8):
            c[s, k] = ahead[k]
        ahead = [column(r[s + 1][at], lane + 8 + k) for k in range(8)] if s < 7 else []
        scale = jnp.zeros((8, 128), F32)
        for j in range(8):
            pivot = row(c[s, j], j)
            inverse = 1.0 / pivot
            scale = jnp.where(sublane == j, lax.rsqrt(pivot), scale)
            across = [row(c[s + 1, j], k) for k in range(len(ahead))]
            for g in range(s, 8):
                c[g, j] = c[g, j] * inverse
            for k in range(len(ahead)):
                ahead[k] = ahead[k] - c[s + 1, j] * across[k]
            below = jnp.where(sublane > j, c[s, j], 0.0)
            for k in range(j + 1, 8):
                across = row(c[s, k], j)
                for g in range(s, 8):
                    c[g, k] = c[g, k] - c[g, j] * across
            for t in range(3):
                across = row(r[s][t], j)
                r[s][t] = r[s][t] - below * across
                for g in range(s + 1, 8):
                    r[g][t] = r[g][t] - c[g, j] * across
        for t in range(3):
            r[s][t] = r[s][t] * scale
    for g in range(8):
        for i, t in enumerate(tiles):
            m[place(g, t)] = r[g][i]
    low = top + 64
    if low < 256:
        width = slice(128 * tiles[0], 128 * tiles[0] + 384)
        hl, ml, ll = pieces(m[top:low, low // 128 * 128 : 256])
        hp, mp, lp = pieces(m[top:low, width])
        update = lax.dot_general(
            jnp.concatenate([hl, hl, ml, ml], axis=0),
            jnp.concatenate([hp, mp, hp, mp], axis=0),
            TN, preferred_element_type=F32,
        )
        update += lax.dot_general(
            jnp.concatenate([hl, ll], axis=0), jnp.concatenate([lp, hp], axis=0), TN, preferred_element_type=F32
        )
        m[low:, width] -= update[low % 128 :]


def deliver(q, r, p, q_hbm, r_hbm, p_hbm, sem):
    copies = [
        pltpu.make_async_copy(src, dst, sem.at[i])
        for i, (src, dst) in enumerate([(q, q_hbm), (r, r_hbm), (p, p_hbm)])
    ]
    for copy in copies:
        copy.start()
    for copy in copies:
        copy.wait()


def local(archive, sketch):
    pixels, depth = archive.shape
    rank = sketch.shape[1]
    root = float(pixels * lax.axis_size("gx") * lax.axis_size("gy")) ** 0.5
    any_spec = pl.BlockSpec(memory_space=pl.ANY)
    vmem = pl.BlockSpec(memory_space=pltpu.VMEM)
    dma = pltpu.SemaphoreType.DMA
    results = pl.pallas_call(
        functools.partial(exchange, root),
        out_shape=(
            pltpu.VMEM((pixels, rank), BF16),
            pltpu.VMEM((rank, rank), F32),
            pltpu.VMEM((4, rank), F32),
        ),
        in_specs=[any_spec, any_spec],
        out_specs=(vmem, vmem, vmem),
        scratch_shapes=[
            pltpu.VMEM((pixels, depth), BF16),
            pltpu.VMEM((depth, rank), BF16),
            pltpu.VMEM((pixels, 2 * rank), BF16),
            pltpu.VMEM((2 * rank, pixels), BF16),
            pltpu.VMEM((32, 8, 256), F32),
            pltpu.VMEM((16, 8, 256), F32),
            pltpu.VMEM((15, 8, 256), F32),
            pltpu.VMEM((8, 8, 256), F32),
            pltpu.VMEM((32, 8, 256), F32),
            pltpu.VMEM((128, 8, 256), F32),
            pltpu.VMEM((64, 8, 256), F32),
            pltpu.VMEM((16, 4, 8, 256), F32),
            pltpu.VMEM((15, 4, 8, 256), F32),
            pltpu.VMEM((4, 8, 256), F32),
            pltpu.VMEM((8, 8, 256), F32),
            pltpu.VMEM((rank, 2 * rank), F32),
            dma((len(SPLIT) - 1,)), dma, dma, dma, dma((15,)), dma((15,)),
            dma((7,)), dma((7,)), dma((15,)), dma((15,)), dma, dma,
            dma, dma, dma((15,)), dma((15,)), dma((8,)), dma((8,)),
        ],
        compiler_params=pltpu.CompilerParams(
            collective_id=0, has_side_effects=True, vmem_limit_bytes=52 * 2**20
        ),
    )(archive, sketch)
    return pl.pallas_call(
        deliver,
        out_shape=tuple(jax.ShapeDtypeStruct(r.shape, r.dtype) for r in results),
        in_specs=[vmem] * 3,
        out_specs=(any_spec,) * 3,
        scratch_shapes=[dma((3,))],
        compiler_params=pltpu.CompilerParams(vmem_limit_bytes=4 * 2**20),
    )(*results)


def solution(mesh):
    return jax.shard_map(
        local,
        mesh=mesh,
        in_specs=(P(("gx", "gy"), None), P()),
        out_specs=(P(("gx", "gy"), None), P(), P(("gx", "gy"), None)),
        check_vma=False,
    )
```

```python
import functools

import jax
import jax.numpy as jnp
from jax import lax
from jax.experimental import pallas as pl
from jax.experimental.pallas import tpu as pltpu
from jax.sharding import PartitionSpec as P

F32, BF16 = jnp.float32, jnp.bfloat16
SPLIT = (0, 2048, 3072, 4096)
CHUNKS = 4
EARLY = 1
MESH = pl.DeviceIdType.MESH
NT = (((1,), (1,)), ((), ()))
TN = (((0,), (0,)), ((), ()))


def dot(a, b):
    return jnp.dot(a, b, preferred_element_type=F32)


def dot_nt(a, b):
    return lax.dot_general(a, b, NT, preferred_element_type=F32)


def pieces(value):
    high = value.astype(BF16)
    rest = value - high.astype(F32)
    middle = rest.astype(BF16)
    return high, middle, (rest - middle.astype(F32)).astype(BF16)


PLANE = sorted(((i // 4, i % 4) for i in range(1, 16)), key=lambda o: -min(o[0], 4 - o[0]) - min(o[1], 4 - o[1]))
LINE = sorted(range(1, 8), key=lambda o: -min(o, 8 - o))


def basis(block, scaled):
    return dot_nt(jnp.concatenate([block, block[:, :256]], axis=1), scaled).astype(BF16)


def exchange(
    root, archive_hbm, sketch_hbm, q_ref, s, scaled_ref, r_ref, p_ref,
    a, sk, hm, g, gcore, gxy, gz, gsum, w, wcore, wtile, wxy, wsum, wz, m,
    a_sem, sk_sem, send1, recv1, send2, recv2, send3, recv3, send4, recv4,
    send5, recv5, wsend1, wrecv1, wsend2, wrecv2, wsend3, wrecv3,
):
    z, gy = lax.axis_index("gx"), lax.axis_index("gy")
    core, xy = gy % 2, gy // 2
    x, y = xy // 4, xy % 4
    other = 1 - core
    chunk = s.shape[0] // CHUNKS
    parts = [slice(i, j) for i, j in zip(SPLIT, SPLIT[1:])]

    def device(zz, xx, cc):
        return (zz, xx * 2 + cc)

    def along(o, sign=1):
        return ((x + sign * o[0] + 4) % 4) * 4 + (y + sign * o[1] + 4) % 4

    def remote(src, dst, send, recv, to):
        return pltpu.make_async_remote_copy(
            src_ref=src, dst_ref=dst, send_sem=send, recv_sem=recv, device_id=to, device_id_type=MESH
        )

    def half(ref, which, size):
        return ref.at[pl.ds(pl.multiple_of(which * size, size), size)]

    def load(i):
        return pltpu.make_async_copy(archive_hbm.at[parts[i]], a.at[parts[i]], a_sem.at[i])

    load_sketch = pltpu.make_async_copy(sketch_hbm, sk, sk_sem)
    load_sketch.start()
    for i in range(len(parts)):
        load(i).start()

    barrier = pltpu.get_barrier_semaphore()
    for o in PLANE:
        pl.semaphore_signal(barrier, inc=1, device_id=device(z, along(o), core), device_id_type=MESH)
    for o in LINE:
        for cc in range(2):
            pl.semaphore_signal(barrier, inc=1, device_id=device((z + o) % 8, xy, cc), device_id_type=MESH)
    sibling = device(z, xy, other)
    pl.semaphore_signal(barrier, inc=1, device_id=sibling, device_id_type=MESH)

    load_sketch.wait()
    for i, part in enumerate(parts):
        load(i).wait()
        high, middle, _ = pieces(dot(a[part], sk[...]))
        block = jnp.concatenate([high, middle], axis=1)
        s[part] = block
        hm[:, part] = block.T

    def gram(which):
        first = pl.multiple_of(which * 128, 128)
        mine = jnp.concatenate([hm[pl.ds(first, 128)], hm[pl.ds(first + 256, 128)]], axis=0)
        four = dot_nt(mine, hm[...])
        four = four[:, :256] + four[:, 256:]
        half(g, which, 16)[...] = (four[:128] + four[128:]).reshape(16, 8, 256)

    def cross(which):
        columns = pl.ds(pl.multiple_of(which * 512, 512), 512)
        both = dot(hm[...], a[:, columns])
        half(w, which, 64)[...] = (both[:256] + both[256:]).T.reshape(64, 8, 256)

    gram(other)
    pl.semaphore_wait(barrier, 30)
    one = remote(half(g, other, 16), gcore, send1, recv1, sibling)
    one.start()
    gram(core)
    one.wait()
    gcore[...] += half(g, core, 16)[...]

    def two(i):
        to = along(PLANE[i])
        return remote(gcore.at[to], gxy.at[i], send2.at[i], recv2.at[i], device(z, to, core))

    for i in range(15):
        two(i).start()
    cross(other)
    wone = remote(half(w, other, 64), wcore, wsend1, wrecv1, sibling)
    wone.start()
    cross(core)
    total = gcore[xy]
    for i in reversed(range(15)):
        two(i).wait_recv()
        total += gxy[i]
    gz[z] = total

    def three(i):
        return remote(gz.at[z], gz.at[z], send3.at[i], recv3.at[i], device((z + LINE[i]) % 8, xy, core))

    def three_in(i):
        slot = (z - LINE[i] + 8) % 8
        return remote(gz.at[slot], gz.at[slot], send3.at[i], recv3.at[i], device(slot, xy, core))

    for i in range(7):
        three(i).start()

    wone.wait()
    for t in range(4):
        for i in range(16):
            wtile[i, t] = wcore[t * 16 + i] + w[core * 64 + t * 16 + i]

    def wtwo(i):
        to = along(PLANE[i])
        return remote(wtile.at[to], wxy.at[i], wsend2.at[i], wrecv2.at[i], device(z, to, core))

    for i in range(15):
        wtwo(i).start()

    for i in reversed(range(7)):
        three_in(i).wait_recv()
    total = gz[0]
    for o in range(1, 8):
        total += gz[o]
    mine = core * 16 + xy
    gsum[mine] = total

    def four(i):
        return remote(gsum.at[mine], gsum.at[mine], send4.at[i], recv4.at[i], device(z, along(PLANE[i]), core))

    def four_in(i):
        slot = along(PLANE[i], -1)
        there = gsum.at[core * 16 + slot]
        return remote(there, there, send4.at[i], recv4.at[i], device(z, slot, core))

    for i in range(15):
        four(i).start()
    for i in reversed(range(15)):
        four_in(i).wait_recv()
    five = remote(half(gsum, core, 16), half(gsum, core, 16), send5, recv5, sibling)
    five_in = remote(half(gsum, other, 16), half(gsum, other, 16), send5, recv5, sibling)
    five.start()
    above = lax.broadcasted_iota(jnp.int32, (256, 256), 1) - lax.broadcasted_iota(jnp.int32, (256, 256), 0)
    m[:, 256:] = jnp.where(above == 0, 1.0, 0.0)

    def wthree(t, cc):
        return remote(
            wsum.at[t], wz.at[z], wsend3.at[t * 2 + cc], wrecv3.at[z], device(core * 4 + t, xy, cc)
        )

    def here(t, cc):
        return jnp.logical_and(z == core * 4 + t, core == cc)

    def along_z():
        total = wtile[xy]
        for i in reversed(range(15)):
            wtwo(i).wait_recv()
            total += wxy[i]
        wsum[...] = total
        for t in range(4):
            for cc in range(2):

                @pl.when(jnp.logical_not(here(t, cc)))
                def _():
                    wthree(t, cc).start()

                @pl.when(here(t, cc))
                def _():
                    wz[z] = wsum[t]

    along_z()
    five_in.wait_recv()
    m[:, :256] = gsum[...].reshape(256, 256)
    for top in range(0, 256, 64):
        factor(m, top)

    inverse = jnp.where(above <= 0, m[:, 256:], 0.0)
    high, middle, _ = pieces(inverse * root)
    scaled_ref[...] = jnp.concatenate([high, high, middle], axis=1)
    for i in range(EARLY):
        q_ref[pl.ds(i * chunk, chunk)] = basis(s[pl.ds(i * chunk, chunk)], scaled_ref[...])
    r_ref[...] = jnp.where(above >= 0, m[:, :256] / root, 0.0)

    owner = z // 4
    for zz in range(8):

        @pl.when(jnp.logical_not(jnp.logical_and(z == zz, core == owner)))
        def _():
            remote(
                wsum.at[0], wz.at[zz], wsend3.at[0], wrecv3.at[zz], device(zz, xy, owner)
            ).wait_recv()

    total = wz[0]
    for zz in range(1, 8):
        total += wz[zz]
    p_ref[...] = lax.dot_general(
        jnp.where(core == 0, total[:4], total[4:]), inverse, NT,
        precision=lax.Precision.HIGHEST, preferred_element_type=F32,
    )

    for i in range(15):
        two(i).wait_send()
        four(i).wait_send()
        wtwo(i).wait_send()
    for i in range(7):
        three(i).wait_send()
    five.wait_send()
    for t in range(4):
        for cc in range(2):

            @pl.when(jnp.logical_not(here(t, cc)))
            def _():
                wthree(t, cc).wait_send()


def row(tile, j):
    return jnp.broadcast_to(tile[j : j + 1, :], (8, 128))


def column(tile, k):
    return jnp.broadcast_to(tile[:, k : k + 1], (8, 128))


def factor(m, top):
    sublane = lax.broadcasted_iota(jnp.int32, (8, 128), 0)
    tiles = [0, 1, 2] if top < 128 else [1, 2, 3]
    at = tiles.index(top // 128)

    def place(g, t):
        return slice(top + 8 * g, top + 8 * g + 8), slice(128 * t, 128 * t + 128)

    r = [[m[place(g, t)] for t in tiles] for g in range(8)]
    ahead = [column(r[0][at], top % 128 + k) for k in range(8)]
    for s in range(8):
        lane = (top + 8 * s) % 128
        c = {(g, k): column(r[g][at], lane + k) for g in range(s + 1, 8) for k in range(8)}
        for k in range(8):
            c[s, k] = ahead[k]
        ahead = [column(r[s + 1][at], lane + 8 + k) for k in range(8)] if s < 7 else []
        scale = jnp.zeros((8, 128), F32)
        for j in range(8):
            pivot = row(c[s, j], j) if j == 0 else following
            inverse = 1.0 / pivot
            scale = jnp.where(sublane == j, lax.rsqrt(pivot), scale)
            own = c[s, j]
            across = [row(c[s + 1, j], k) for k in range(len(ahead))]
            for g in range(s, 8):
                c[g, j] = c[g, j] * inverse
            for k in range(len(ahead)):
                ahead[k] = ahead[k] - c[s + 1, j] * across[k]
            below = jnp.where(sublane > j, c[s, j], 0.0)
            if j < 7:
                across = row(c[s, j + 1], j)
                following = row(c[s, j + 1], j + 1) - across * across * inverse
            for k in range(j + 1, 8):
                across = row(c[s, k], j)
                c[s, k] = c[s, k] - own * across * inverse
                for g in range(s + 1, 8):
                    c[g, k] = c[g, k] - c[g, j] * across
            for t in range(3):
                across = row(r[s][t], j)
                r[s][t] = r[s][t] - below * across
                for g in range(s + 1, 8):
                    r[g][t] = r[g][t] - c[g, j] * across
        for t in range(3):
            r[s][t] = r[s][t] * scale
    for g in range(8):
        for i, t in enumerate(tiles):
            m[place(g, t)] = r[g][i]
    low = top + 64
    if low < 256:
        width = slice(128 * tiles[0], 128 * tiles[0] + 384)
        hl, ml, ll = pieces(m[top:low, low // 128 * 128 : 256])
        hp, mp, lp = pieces(m[top:low, width])
        update = lax.dot_general(
            jnp.concatenate([hl, hl, ml, ml], axis=0),
            jnp.concatenate([hp, mp, hp, mp], axis=0),
            TN, preferred_element_type=F32,
        )
        update += lax.dot_general(
            jnp.concatenate([hl, ll], axis=0), jnp.concatenate([lp, hp], axis=0), TN, preferred_element_type=F32
        )
        m[low:, width] -= update[low % 128 :]


def deliver(q, s, scaled, r, p, q_hbm, r_hbm, p_hbm, late, sem):
    chunk = s.shape[0] // CHUNKS

    def save(i):
        src = q.at[pl.ds(i * chunk, chunk)] if i < EARLY else late.at[i - EARLY]
        return pltpu.make_async_copy(src, q_hbm.at[pl.ds(i * chunk, chunk)], sem.at[i])

    pass_r = pltpu.make_async_copy(r, r_hbm, sem.at[CHUNKS])
    pass_p = pltpu.make_async_copy(p, p_hbm, sem.at[CHUNKS + 1])
    for i in range(EARLY):
        save(i).start()
    pass_r.start()
    pass_p.start()
    for i in range(EARLY, CHUNKS):
        late[i - EARLY] = basis(s[pl.ds(i * chunk, chunk)], scaled[...])
        save(i).start()
    for i in range(CHUNKS):
        save(i).wait()
    pass_r.wait()
    pass_p.wait()


def local(archive, sketch):
    pixels, depth = archive.shape
    rank = sketch.shape[1]
    chunk = pixels // CHUNKS
    root = float(pixels * lax.axis_size("gx") * lax.axis_size("gy")) ** 0.5
    any_spec = pl.BlockSpec(memory_space=pl.ANY)
    vmem = pl.BlockSpec(memory_space=pltpu.VMEM)
    dma = pltpu.SemaphoreType.DMA
    results = pl.pallas_call(
        functools.partial(exchange, root),
        out_shape=(
            pltpu.VMEM((EARLY * chunk, rank), BF16),
            pltpu.VMEM((pixels, 2 * rank), BF16),
            pltpu.VMEM((rank, 3 * rank), BF16),
            pltpu.VMEM((rank, rank), F32),
            pltpu.VMEM((4, rank), F32),
        ),
        in_specs=[any_spec, any_spec],
        out_specs=(vmem,) * 5,
        scratch_shapes=[
            pltpu.VMEM((pixels, depth), BF16),
            pltpu.VMEM((depth, rank), BF16),
            pltpu.VMEM((2 * rank, pixels), BF16),
            pltpu.VMEM((32, 8, 256), F32),
            pltpu.VMEM((16, 8, 256), F32),
            pltpu.VMEM((15, 8, 256), F32),
            pltpu.VMEM((8, 8, 256), F32),
            pltpu.VMEM((32, 8, 256), F32),
            pltpu.VMEM((128, 8, 256), F32),
            pltpu.VMEM((64, 8, 256), F32),
            pltpu.VMEM((16, 4, 8, 256), F32),
            pltpu.VMEM((15, 4, 8, 256), F32),
            pltpu.VMEM((4, 8, 256), F32),
            pltpu.VMEM((8, 8, 256), F32),
            pltpu.VMEM((rank, 2 * rank), F32),
            dma((len(SPLIT) - 1,)), dma, dma, dma, dma((15,)), dma((15,)),
            dma((7,)), dma((7,)), dma((15,)), dma((15,)), dma, dma,
            dma, dma, dma((15,)), dma((15,)), dma((8,)), dma((8,)),
        ],
        compiler_params=pltpu.CompilerParams(
            collective_id=0, has_side_effects=True, vmem_limit_bytes=52 * 2**20
        ),
    )(archive, sketch)
    return pl.pallas_call(
        deliver,
        out_shape=(
            jax.ShapeDtypeStruct((pixels, rank), BF16),
            jax.ShapeDtypeStruct((rank, rank), F32),
            jax.ShapeDtypeStruct((4, rank), F32),
        ),
        in_specs=[vmem] * 5,
        out_specs=(any_spec,) * 3,
        scratch_shapes=[pltpu.VMEM((CHUNKS - EARLY, chunk, rank), BF16), dma((CHUNKS + 2,))],
        compiler_params=pltpu.CompilerParams(vmem_limit_bytes=8 * 2**20),
    )(*results)


def solution(mesh):
    return jax.shard_map(
        local,
        mesh=mesh,
        in_specs=(P(("gx", "gy"), None), P()),
        out_specs=(P(("gx", "gy"), None), P(), P(("gx", "gy"), None)),
        check_vma=False,
    )
```
